128 devices in a mesh: gallery: 32 (over x, y, core), query: 4 (over z).
Axes of the slice: x: 4, y: 4, z: 4, core: 2. Of those that a mesh axis runs over, the one named last changes fastest.
Arguments:
- text_states: bfloat16 [4096, 32, 768], P(('gallery', 'query')), may hold values from -50 to 50
- caption_aligned_vector: bfloat16 [4096, 256], P(('gallery', 'query')), may hold values from -0.375 to 0.375
- cluster_list: int32 [4096, 8], P(('gallery', 'query')), may hold values from 0 to 255
- pair_image: int32 [4096, 16], P(('gallery', 'query')), may hold values from 0 to 511, as said below
- image_keys: bfloat16 [512, 577, 768], P(('gallery', 'query')), may hold values from -368 to 368
- image_values: bfloat16 [512, 577, 768], P(('gallery', 'query')), may hold values from -6 to 6
- picture_aligned_vector: bfloat16 [512, 256], P(('gallery', 'query')), may hold values from -6 to 6
- w_self_q: bfloat16 [768, 768], replicated, may hold values from -0.21875 to 0.21875
- w_self_k: bfloat16 [768, 768], replicated, may hold values from -0.21875 to 0.21875
- w_self_v: bfloat16 [768, 768], replicated, may hold values from -0.21875 to 0.21875
- w_self_o: bfloat16 [768, 768], replicated, may hold values from -0.21875 to 0.21875
- w_cross_q: bfloat16 [768, 768], replicated, may hold values from -0.21875 to 0.21875
- w_cross_o: bfloat16 [768, 768], replicated, may hold values from -0.21875 to 0.21875
- w_up: bfloat16 [768, 3072], replicated, may hold values from -0.21875 to 0.21875
- w_down: bfloat16 [3072, 768], replicated, may hold values from -0.109375 to 0.109375
- itm_head: bfloat16 [768, 2], replicated, may hold values from -0.21875 to 0.21875
Outputs:
- rerank: float32 [4096, 16], P(('gallery', 'query'))
The draws below stay inside these ranges and needn't reach their ends.
Inputs may be any that keep to these rules, and one draw needn't show every extreme that they name: `pair_image`: images j * 4 to (j + 1) * 4 - 1 form shard j. Among the 512 pairs of the queries n * 32 to (n + 1) * 32 - 1, at most 5 have their image in any one shard, and in every draw one shard holds exactly 5 of them for every n. A query may name an image twice.
All inputs are finite; a program needn't handle non-finite values.
Results may differ from the reference program's by a relative error of at most 0.0024.
Values may be sent and summed in bfloat16 or wider, within the bound.
A program may use at most 256 MiB of HBM per device.

```python
import jax
import jax.numpy as jnp
from jax import lax

D = 768
HEADS = 12
FF = 3072
E = 256
HEAD = 64
TLEN = 32
IMG_TOK = 577
TOPK = 16
NLIST = 8
BLOCK_IMG = 2
Q_DEV = 32
IMG_DEV = 4
QUERIES = 4096
IMAGES = 512
BLOCKS = 256
CAP = 5


def shared_itc(key):
    text_offset_start = jnp.clip(jax.random.normal(jax.random.fold_in(key, 101), (QUERIES, E), jnp.float32), -6.0, 6.0) * 0.0625
    image_base = jnp.clip(jax.random.normal(jax.random.fold_in(key, 102), (IMAGES, E), jnp.float32), -6.0, 6.0) * 0.0625
    return (text_offset_start, image_base)


def draw_caption_aligned_vector(key, part):
    text_offset_start, image_base = shared_itc(key)
    return text_offset_start.astype(jnp.bfloat16)


def draw_picture_aligned_vector(key, part):
    text_offset_start, image_base = shared_itc(key)
    return image_base.astype(jnp.bfloat16)


def draw_text_states(key, part):
    key = jax.random.fold_in(key, 3)
    text_offset_start = jnp.clip(jax.random.normal(key, (QUERIES, TLEN, D), jnp.float32), -6.0, 6.0)
    return text_offset_start.astype(jnp.bfloat16)


def draw_image_keys(key, part):
    key = jax.random.fold_in(key, 7)
    key_base = jnp.clip(jax.random.normal(key, (IMAGES, IMG_TOK, D), jnp.float32), -6.0, 6.0)
    return key_base.astype(jnp.bfloat16)


def draw_pair_image(key, part):
    key = jax.random.fold_in(key, 11)
    device_total = IMAGES // IMG_DEV
    pair_total = Q_DEV * TOPK
    key_hot, key_owner, key_local = jax.random.split(key, 3)
    hot_owner = jax.random.randint(key_hot, (), 0, device_total)
    rest_pool = jnp.arange((device_total - 1) * CAP) // CAP
    rest_pool = rest_pool + (rest_pool >= hot_owner).astype(rest_pool.dtype)

    def device_owners(device_key):
        key_pool, key_order = jax.random.split(device_key)
        shuffled = jax.random.permutation(key_pool, rest_pool)
        sequence = jnp.concatenate([jnp.full((CAP,), hot_owner, dtype=shuffled.dtype), shuffled])[:pair_total]
        return jax.random.permutation(key_order, sequence)
    owners = jax.vmap(device_owners)(jax.random.split(key_owner, device_total))
    local_pick = jax.random.randint(key_local, (device_total, pair_total), 0, IMG_DEV)
    return (owners * IMG_DEV + local_pick).reshape(QUERIES, TOPK).astype(jnp.int32)


def with_ends(array, rng, smallest, largest):
    dims = array.shape
    index_at = [jax.random.randint(jax.random.fold_in(rng, axis), (), 0, dims[axis]) for axis in range(len(dims))]
    array = array.at[tuple(index_at)].set(smallest)
    longest = dims.index(max(dims))
    index_at[longest] = (index_at[longest] + 1) % dims[longest]
    return array.at[tuple(index_at)].set(largest)


def block_scale(key, extent, cuts, least, high):
    gain, own = 1.0, jax.random.fold_in(key, 6)
    for axis_at, blocks in cuts:
        heights = jnp.exp(jax.random.uniform(jax.random.fold_in(own, axis_at), (blocks,), jnp.float32, least / len(cuts), high / len(cuts)))
        gain = gain * jnp.repeat(heights, extent[axis_at] // blocks).reshape([-1 if axis == axis_at else 1 for axis in range(len(extent))])
    return gain


def scatter_about(key, extent, width, limit, cuts=(), kind=jnp.bfloat16):
    drawn = width * jax.random.normal(key, extent, jnp.float32)
    if cuts:
        drawn = drawn * block_scale(key, extent, cuts, -0.22, 0.18)
    return jnp.clip(drawn, -limit, limit).astype(kind)


def setup_inputs(seed: int = 0) -> dict:
    arg_keys = jax.random.split(jax.random.key(seed), 17)
    return {
        "text_states": draw_text_states(jax.random.fold_in(arg_keys[16], 71), 0),
        "caption_aligned_vector": draw_caption_aligned_vector(jax.random.fold_in(arg_keys[16], 71), 0),
        "cluster_list": with_ends(jax.random.randint(arg_keys[2], (QUERIES, NLIST), 0, BLOCKS), jax.random.fold_in(arg_keys[2], 1), 0, BLOCKS - 1).astype(jnp.int32),
        "pair_image": draw_pair_image(jax.random.fold_in(arg_keys[16], 71), 0),
        "image_keys": draw_image_keys(jax.random.fold_in(arg_keys[16], 71), 0),
        "image_values": scatter_about(arg_keys[5], (IMAGES, IMG_TOK, D), 1.0, 6.0, ((0, 128),)),
        "picture_aligned_vector": draw_picture_aligned_vector(jax.random.fold_in(arg_keys[16], 71), 0),
        "w_self_q": scatter_about(arg_keys[7], (D, D), D ** -0.5, 0.21875),
        "w_self_k": scatter_about(arg_keys[8], (D, D), D ** -0.5, 0.21875),
        "w_self_v": scatter_about(arg_keys[9], (D, D), D ** -0.5, 0.21875),
        "w_self_o": scatter_about(arg_keys[10], (D, D), D ** -0.5, 0.21875),
        "w_cross_q": scatter_about(arg_keys[11], (D, D), D ** -0.5, 0.21875),
        "w_cross_o": scatter_about(arg_keys[12], (D, D), D ** -0.5, 0.21875),
        "w_up": scatter_about(arg_keys[13], (D, FF), D ** -0.5, 0.21875),
        "w_down": scatter_about(arg_keys[14], (FF, D), FF ** -0.5, 0.109375),
        "itm_head": scatter_about(arg_keys[15], (D, 2), D ** -0.5, 0.21875),
    }


norm_epsilon = 1e-06
inverse_softness_factor = 1.0 / 0.07

def layer_norm(inputs):
    centered = inputs - lax.optimization_barrier(jnp.mean(inputs, axis=-1, keepdims=True))
    variance = lax.optimization_barrier(jnp.mean(centered * centered, axis=-1, keepdims=True))
    return centered * lax.rsqrt(variance + norm_epsilon)

def upcast_precise(downcast_compact):
    return lax.optimization_barrier(downcast_compact).astype(jnp.float32)

def itm_logits(state, w_up, w_down, itm_head):
    hidden = jax.nn.gelu(jnp.dot(state, w_up, preferred_element_type=jnp.float32), approximate=False).astype(jnp.bfloat16)
    mixed_state = layer_norm(state.astype(jnp.float32) + jnp.dot(hidden, w_down, preferred_element_type=jnp.float32)).astype(jnp.bfloat16)
    return jnp.dot(mixed_state, itm_head, preferred_element_type=jnp.float32)

def summary_focus_weights(text_states, w_self_q, w_self_k, w_self_v, w_self_o):
    query_total, text_length, features = text_states.shape
    first_token = text_states[:, 0, :]
    cls_query = upcast_precise(jnp.dot(first_token, w_self_q, preferred_element_type=jnp.float32).astype(jnp.bfloat16))
    flat_rows = text_states.reshape(query_total * text_length, features)
    key_rows = upcast_precise(jnp.dot(flat_rows, w_self_k, preferred_element_type=jnp.float32).astype(jnp.bfloat16))
    value_rows = upcast_precise(jnp.dot(flat_rows, w_self_v, preferred_element_type=jnp.float32).astype(jnp.bfloat16))
    cls_query = cls_query.reshape(query_total, HEADS, HEAD)
    key_rows = key_rows.reshape(query_total, text_length, HEADS, HEAD)
    value_rows = value_rows.reshape(query_total, text_length, HEADS, HEAD)
    scores = jnp.einsum('nhd,nthd->nht', cls_query, key_rows) * HEAD ** (-0.5)
    weights = upcast_precise(jax.nn.softmax(scores, axis=-1).astype(jnp.bfloat16))
    context = jnp.einsum('nht,nthd->nhd', weights, value_rows).astype(jnp.bfloat16).reshape(query_total, features)
    attended = jnp.dot(context, w_self_o, preferred_element_type=jnp.float32)
    return layer_norm(first_token.astype(jnp.float32) + attended).astype(jnp.bfloat16)

def reference(text_states, caption_aligned_vector, cluster_list, pair_image, image_keys, image_values, picture_aligned_vector, w_self_q, w_self_k, w_self_v, w_self_o, w_cross_q, w_cross_o, w_up, w_down, itm_head):
    leading_token_state = summary_focus_weights(text_states, w_self_q, w_self_k, w_self_v, w_self_o)
    similarity_logit_matrix = jnp.dot(caption_aligned_vector, picture_aligned_vector.T, preferred_element_type=jnp.float32) * inverse_softness_factor
    block_index = (jnp.arange(IMAGES) // BLOCK_IMG).astype(jnp.int32)
    listed = jnp.any(cluster_list[:, :, None] == block_index[None, None, :], axis=1)
    masked = jnp.where(listed, similarity_logit_matrix, -1e+30)
    top_value = lax.optimization_barrier(jnp.max(masked, axis=1))
    total_sum = lax.optimization_barrier(jnp.sum(jnp.where(listed, jnp.exp(masked - top_value[:, None]), 0.0), axis=1))
    itc_total = top_value + jnp.log(total_sum)
    pair_itc = jnp.take_along_axis(similarity_logit_matrix, pair_image.astype(jnp.int32), axis=1)
    block_pairs = 8 * TOPK
    image_ids = pair_image.astype(jnp.int32).reshape(-1, block_pairs)
    query_ids = (jnp.arange(QUERIES * TOPK) // TOPK).astype(jnp.int32).reshape(-1, block_pairs)

    def margin_block(image_item):
        images, queries = image_item
        state = leading_token_state[queries]
        cross_query = upcast_precise(jnp.dot(state, w_cross_q, preferred_element_type=jnp.float32).astype(jnp.bfloat16))
        cross_query = cross_query.reshape(block_pairs, HEADS, HEAD)
        key_rows = image_keys[images].astype(jnp.float32).reshape(block_pairs, IMG_TOK, HEADS, HEAD)
        value_rows = image_values[images].astype(jnp.float32).reshape(block_pairs, IMG_TOK, HEADS, HEAD)
        scores = jnp.einsum('bhd,bthd->bht', cross_query, key_rows) * HEAD ** (-0.5)
        weights = upcast_precise(jax.nn.softmax(scores, axis=-1).astype(jnp.bfloat16))
        context = jnp.einsum('bht,bthd->bhd', weights, value_rows).astype(jnp.bfloat16).reshape(block_pairs, D)
        cross_state = layer_norm(state.astype(jnp.float32) + jnp.dot(context, w_cross_o, preferred_element_type=jnp.float32)).astype(jnp.bfloat16)
        logits = itm_logits(cross_state, w_up, w_down, itm_head)
        return logits[:, 1] - logits[:, 0]
    margin = lax.map(margin_block, (image_ids, query_ids)).reshape(QUERIES, TOPK)
    return margin + pair_itc - itc_total[:, None]
```

```python
import functools

import jax
import jax.numpy as jnp
from jax import lax
from jax.experimental import pallas as pl
from jax.experimental.pallas import tpu as pltpu
from jax.sharding import PartitionSpec as P

F32 = jnp.float32
BF16 = jnp.bfloat16
MESH = pl.DeviceIdType.MESH

HEADS = 12
HEAD = 64
D = 768
FF = 3072
TLEN = 32
Q_DEV = 32
TOPK = 16
IMG_DEV = 4
IMG_TOK = 577
CAP = 5
DEVICES = 128
MEMBERS = 4
PAIRS = Q_DEV * TOPK
SLOTS = DEVICES * CAP
CHUNKS = D // 128
BLOCK = 32
INFO = CAP * CHUNKS
TILE = 64
SORTED = SLOTS + (IMG_DEV - 1) * TILE
GROUP = 256
FF_STEP = 256

norm_epsilon = 1e-06
inverse_softness_factor = 1.0 / 0.07
VMEM_LIMIT = 56 * 1024 * 1024


def iota(shape, dimension):
    return lax.broadcasted_iota(jnp.int32, shape, dimension)


def dot(left, right, left_dim=1, right_dim=0):
    return lax.dot_general(
        left, right, (((left_dim,), (right_dim,)), ((), ())), preferred_element_type=F32
    )


def layer_norm(inputs):
    centered = inputs - jnp.mean(inputs, axis=-1, keepdims=True)
    variance = jnp.mean(centered * centered, axis=-1, keepdims=True)
    return centered * lax.rsqrt(variance + norm_epsilon)


def gelu(x):
    z = jnp.abs(x) * 0.7071067811865476
    t = 1.0 / (1.0 + 0.3275911 * z)
    poly = t * (
        0.254829592
        + t * (-0.284496736 + t * (1.421413741 + t * (-1.453152027 + t * 1.061405429)))
    )
    half_tail = 0.5 * poly * jnp.exp(-z * z)
    return x * jnp.where(x < 0, half_tail, 1.0 - half_tail)


def pair_columns(pair_ref):
    pairs = pair_ref[...]
    spread = (iota((PAIRS, Q_DEV), 0) // TOPK == iota((PAIRS, Q_DEV), 1)).astype(BF16)
    place = iota((PAIRS, TOPK), 0) % TOPK == iota((PAIRS, TOPK), 1)

    def column(values):
        rows = dot(spread, values.astype(F32).astype(BF16))
        return jnp.sum(jnp.where(place, rows, 0.0), axis=1, keepdims=True)

    return column(pairs // IMG_DEV), column(pairs % IMG_DEV)


def self_kernel(
    pair_ref, text_hbm, wq_hbm, wk_hbm, wv_hbm, wo_hbm, send_ref, meta_ref,
    text, wq, wk, wv, wo, first, wide, sems,
):
    copies = [
        pltpu.make_async_copy(source, target, sems.at[number])
        for number, (source, target) in enumerate(
            ((text_hbm, text), (wq_hbm, wq), (wk_hbm, wk), (wv_hbm, wv), (wo_hbm, wo))
        )
    ]
    for copy in copies:
        copy.start()

    owner, pick = pair_columns(pair_ref)
    lane = iota((PAIRS, DEVICES), 1)
    owner_marks = lane == owner.astype(jnp.int32)
    owner_hot = owner_marks.astype(F32).astype(BF16)
    earlier = (iota((PAIRS, PAIRS), 1) < iota((PAIRS, PAIRS), 0)).astype(BF16)
    counts = dot(earlier, owner_hot)
    rank = jnp.sum(jnp.where(owner_marks, counts, 0.0), axis=1, keepdims=True)
    meta_ref[...] = jnp.where(lane == 0, owner, jnp.where(lane == 1, rank, 0.0))
    rank_int = rank.astype(jnp.int32)
    query_lane = iota((PAIRS, 256), 1)
    query_of = iota((PAIRS, 256), 0) // TOPK
    query_hot = (query_lane == rank_int * Q_DEV + query_of) & (rank_int < CAP)
    slot_query = dot(owner_hot, query_hot.astype(F32).astype(BF16), 0, 0).astype(BF16)
    pick_hot = jnp.where(lane == rank_int, pick + 1.0, 0.0).astype(BF16)
    slot_pick = dot(owner_hot, pick_hot, 0, 0)
    wide[pl.ds(INFO, DEVICES, stride=BLOCK), :] = slot_pick
    wide[pl.ds(INFO + 1, DEVICES, stride=BLOCK), :] = jnp.zeros((DEVICES, 128), F32)

    copies[0].wait()
    for n in range(Q_DEV):
        first[n : n + 1, :] = text[n * TLEN : n * TLEN + 16, :].astype(F32)[0:1, :]
    first_rows = first[...]
    copies[1].wait()
    query = dot(first_rows.astype(BF16), wq[...]).astype(BF16).astype(F32) * HEAD**-0.5
    copies[2].wait()
    copies[3].wait()
    head_mask = iota((16, D), 1) // HEAD == iota((16, D), 0)
    per_group = GROUP // TLEN
    own = iota((per_group * 16, GROUP), 0) // 16 == iota((per_group * 16, GROUP), 1) // TLEN
    contexts = []
    for group in range(Q_DEV // per_group):
        rows = text[group * GROUP : (group + 1) * GROUP, :]
        keys = dot(rows, wk[...]).astype(BF16)
        values = dot(rows, wv[...]).astype(BF16)
        part = query[group * per_group : (group + 1) * per_group, :]
        spread = jnp.where(head_mask[None], part[:, None, :], 0.0)
        spread = spread.reshape(per_group * 16, D).astype(BF16)
        scores = jnp.where(own, dot(spread, keys, 1, 1), -1e30)
        exps = jnp.exp(scores - jnp.max(scores, axis=1, keepdims=True))
        weights = (exps / jnp.sum(exps, axis=1, keepdims=True)).astype(BF16)
        mixed = dot(weights, values).reshape(per_group, 16, D)
        contexts.append(jnp.sum(jnp.where(head_mask[None], mixed, 0.0), axis=1))
    context = jnp.concatenate(contexts, axis=0).astype(BF16)
    copies[4].wait()
    state = layer_norm(first_rows + dot(context, wo[...])).astype(BF16)
    for slot in range(CAP):
        rows = dot(slot_query[:, slot * Q_DEV : (slot + 1) * Q_DEV], state)
        for chunk in range(CHUNKS):
            wide[pl.ds(slot * CHUNKS + chunk, DEVICES, stride=BLOCK), :] = rows[
                :, chunk * 128 : (chunk + 1) * 128
            ]
    send_ref[...] = wide[...].astype(BF16)


def partner(step):
    me = lax.axis_index("gallery") * MEMBERS + lax.axis_index("query")
    other = (me + step) % DEVICES
    return me, other, (other // MEMBERS, other % MEMBERS)


def greet_all():
    barrier = pltpu.get_barrier_semaphore()

    def greet(step, carry):
        _, _, place = partner(step)
        pl.semaphore_signal(barrier, inc=1, device_id=place, device_id_type=MESH)
        return carry

    lax.fori_loop(1, DEVICES, greet, 0)
    pl.semaphore_wait(barrier, DEVICES - 1)


def exchange_kernel(send_ref, got_ref, own_sem, send_sem, got_sem):
    me, _, _ = partner(0)
    mine = pl.ds(pl.multiple_of(me * BLOCK, BLOCK), BLOCK)
    own = pltpu.make_async_copy(send_ref.at[mine, :], got_ref.at[mine, :], own_sem)
    own.start()
    greet_all()

    def push(step, carry):
        _, other, place = partner(step)
        theirs = pl.ds(pl.multiple_of(other * BLOCK, BLOCK), BLOCK)
        pltpu.make_async_remote_copy(
            src_ref=send_ref.at[theirs, :],
            dst_ref=got_ref.at[mine, :],
            send_sem=send_sem,
            recv_sem=got_sem,
            device_id=place,
            device_id_type=MESH,
        ).start()
        return carry

    lax.fori_loop(1, DEVICES, push, 0)
    own.wait()
    most = pl.ds(0, (DEVICES - 1) * BLOCK)
    pltpu.make_async_copy(send_ref.at[most, :], send_ref.at[most, :], send_sem).wait()
    pltpu.make_async_copy(got_ref.at[most, :], got_ref.at[most, :], got_sem).wait()


def cross_kernel(
    got_ref, head_ref, keys_hbm, values_hbm, wcq_hbm, wco_hbm, up_hbm, down_hbm, out_ref,
    wcq, wco, up, down, keys, values, wide, state, asked, context, hidden, total, sems,
):
    sources = [(wcq_hbm, wcq)]
    for image in range(IMG_DEV):
        sources.append((keys_hbm.at[image], keys.at[image]))
        sources.append((values_hbm.at[image], values.at[image]))
    sources += [(wco_hbm, wco), (up_hbm, up), (down_hbm, down)]
    copies = [
        pltpu.make_async_copy(source, target, sems.at[number])
        for number, (source, target) in enumerate(sources)
    ]
    for copy in copies:
        copy.start()

    wide[...] = got_ref[...].astype(F32)
    for slot in range(CAP):
        for chunk in range(CHUNKS):
            rows = wide[pl.ds(slot * CHUNKS + chunk, DEVICES, stride=BLOCK), :]
            state[
                slot * DEVICES : (slot + 1) * DEVICES, chunk * 128 : (chunk + 1) * 128
            ] = rows.astype(BF16)
    info = wide[pl.ds(INFO, DEVICES, stride=BLOCK), :]
    image = jnp.concatenate([info[:, slot : slot + 1] for slot in range(CAP)], axis=0)
    image = image.astype(jnp.int32) - 1

    lane = iota((SLOTS, 128), 1)
    image_marks = lane == image
    image_hot = image_marks.astype(F32).astype(BF16)
    earlier = (iota((SLOTS, SLOTS), 1) < iota((SLOTS, SLOTS), 0)).astype(F32).astype(BF16)
    counts = dot(earlier, image_hot)
    sizes = jnp.sum(image_marks.astype(F32), axis=0, keepdims=True)
    tiles = (sizes.astype(jnp.int32) + (TILE - 1)) // TILE
    tiles = jnp.broadcast_to(tiles.astype(F32), (8, 128)).astype(BF16)
    before = (iota((128, 128), 0) < iota((128, 128), 1)).astype(F32).astype(BF16)
    starts = dot(tiles, before)[0:1, :]
    target = jnp.sum(
        jnp.where(image_marks, counts + starts * TILE, 0.0), axis=1, keepdims=True
    )
    target = jnp.where(image >= 0, target, -1.0).astype(jnp.int32)
    order = (iota((SLOTS, SORTED), 1) == target).astype(F32).astype(BF16)
    start_at = [
        jnp.sum(jnp.where(iota((1, 128), 1) == number, starts, 0.0)).astype(jnp.int32)
        for number in range(1, IMG_DEV + 1)
    ]

    copies[0].wait()
    query = (dot(state[...], wcq[...]).astype(BF16).astype(F32) * HEAD**-0.5).astype(BF16)
    asked[...] = dot(order, query, 0, 0).astype(BF16)
    for copy in copies[1 : 1 + 2 * IMG_DEV]:
        copy.wait()

    lane_head = iota((1, 256), 1) // HEAD
    context[...] = jnp.zeros_like(context)

    def attend(tile, carry):
        number = sum((tile >= start).astype(jnp.int32) for start in start_at[:-1])
        rows = pl.ds(pl.multiple_of(tile * TILE, TILE), TILE)
        for group in range(D // 256):
            columns = slice(group * 256, (group + 1) * 256)
            part = asked[rows, columns].astype(F32)
            spread = jnp.concatenate(
                [jnp.where(lane_head == head, part, 0.0) for head in range(4)], axis=0
            ).astype(BF16)
            scores = dot(spread, keys[number, :, columns], 1, 1)
            exps = jnp.exp(scores - jnp.max(scores, axis=1, keepdims=True))
            weight = 1.0 / jnp.sum(exps, axis=1, keepdims=True)
            mixed = dot(exps.astype(BF16), values[number, :, columns]) * weight
            joined = jnp.where(lane_head == 0, mixed[:TILE, :], 0.0)
            for head in range(1, 4):
                joined = jnp.where(
                    lane_head == head, mixed[head * TILE : (head + 1) * TILE, :], joined
                )
            context[rows, columns] = joined.astype(BF16)
        return carry

    lax.fori_loop(0, start_at[-1], attend, 0)

    found = dot(order, context[...]).astype(BF16)
    for copy in copies[1 + 2 * IMG_DEV :]:
        copy.wait()
    crossed = layer_norm(state[...].astype(F32) + dot(found, wco[...]))
    state[...] = crossed.astype(BF16)
    total[...] = crossed.astype(BF16).astype(F32)
    steps = FF // FF_STEP

    def raise_step(step):
        columns = pl.ds(pl.multiple_of(step * FF_STEP, FF_STEP), FF_STEP)
        return gelu(dot(state[...], up[:, columns])).astype(BF16)

    def lower_step(step):
        rows = pl.ds(pl.multiple_of(step * FF_STEP, FF_STEP), FF_STEP)
        return dot(hidden[step % 2], down[rows, :])

    hidden[0] = raise_step(0)

    def feed(step, carry):
        total[...] += lower_step(step - 1)
        hidden[step % 2] = raise_step(step)
        return carry

    lax.fori_loop(1, steps, feed, 0)
    final = layer_norm(total[...] + lower_step(steps - 1)).astype(BF16)
    logits = dot(final, head_ref[...])
    margin = logits[:, 1:2] - logits[:, 0:1]
    back = jnp.zeros((DEVICES, 128), F32)
    back_lane = iota((DEVICES, 128), 1)
    for slot in range(CAP):
        back = jnp.where(
            back_lane == slot, margin[slot * DEVICES : (slot + 1) * DEVICES, :], back
        )
    out_ref[...] = back


def return_kernel(
    back_ref, meta_ref, caption_ref, list_ref, pair_ref, picture_ref, out_ref,
    got, own_sem, send_sem, got_sem,
):
    me, _, _ = partner(0)
    own = pltpu.make_async_copy(back_ref.at[me], got.at[me], own_sem)
    own.start()
    greet_all()

    def push(step, carry):
        _, other, place = partner(step)
        pltpu.make_async_remote_copy(
            src_ref=back_ref.at[other],
            dst_ref=got.at[me],
            send_sem=send_sem,
            recv_sem=got_sem,
            device_id=place,
            device_id_type=MESH,
        ).start()
        return carry

    lax.fori_loop(1, DEVICES, push, 0)

    scores = dot(caption_ref[...], picture_ref[...], 1, 1) * inverse_softness_factor
    images = scores.shape[1]
    image = iota((Q_DEV, images), 1)
    lists = list_ref[...]
    listed = image // 2 == lists[:, 0:1]
    for number in range(1, lists.shape[1]):
        listed = listed | (image // 2 == lists[:, number : number + 1])
    masked = jnp.where(listed, scores, -1e30)
    top = jnp.max(masked, axis=1, keepdims=True)
    sums = jnp.sum(jnp.where(listed, jnp.exp(masked - top), 0.0), axis=1, keepdims=True)
    itc_total = top + jnp.log(sums)
    pairs = pair_ref[...]
    pair_lane = iota((Q_DEV, TOPK), 1)
    offset = jnp.zeros((Q_DEV, TOPK), F32)
    for number in range(TOPK):
        chosen = jnp.sum(
            jnp.where(image == pairs[:, number : number + 1], scores, 0.0),
            axis=1,
            keepdims=True,
        )
        offset = jnp.where(pair_lane == number, chosen, offset)
    offset = offset - itc_total

    lane = iota((PAIRS, DEVICES), 1)
    meta = meta_ref[...]
    owner_hot = (lane == meta[:, 0:1].astype(jnp.int32)).astype(F32).astype(BF16)
    slot_marks = lane == meta[:, 1:2].astype(jnp.int32)
    place = iota((PAIRS, 128), 0) % TOPK == iota((PAIRS, 128), 1)

    own.wait()
    most = pl.ds(0, DEVICES - 1)
    pltpu.make_async_copy(back_ref.at[most], back_ref.at[most], send_sem).wait()
    pltpu.make_async_copy(got.at[most], got.at[most], got_sem).wait()
    rest = got[...].reshape(DEVICES, 128)
    chosen = jnp.zeros((PAIRS, 128), F32)
    for _ in range(3):
        piece = rest.astype(BF16)
        chosen = chosen + dot(owner_hot, piece)
        rest = rest - piece.astype(F32)
    margin = jnp.sum(jnp.where(slot_marks, chosen, 0.0), axis=1, keepdims=True)
    placed = jnp.where(place, margin, 0.0).reshape(Q_DEV, TOPK, 128)
    out_ref[...] = jnp.sum(placed, axis=1)[:, :TOPK] + offset


VMEM = pl.BlockSpec(memory_space=pltpu.VMEM)
ANY = pl.BlockSpec(memory_space=pl.ANY)


def local(
    text_states,
    caption_aligned_vector,
    cluster_list,
    pair_image,
    image_keys,
    image_values,
    picture_aligned_vector,
    w_self_q,
    w_self_k,
    w_self_v,
    w_self_o,
    w_cross_q,
    w_cross_o,
    w_up,
    w_down,
    itm_head,
):
    pictures = lax.all_gather(
        picture_aligned_vector, ("gallery", "query"), axis=0, tiled=True
    )
    plain = pltpu.CompilerParams(vmem_limit_bytes=VMEM_LIMIT)
    send, meta = pl.pallas_call(
        self_kernel,
        out_shape=(
            jax.ShapeDtypeStruct((DEVICES * BLOCK, 128), BF16),
            jax.ShapeDtypeStruct((PAIRS, 128), F32),
        ),
        in_specs=[VMEM] + [ANY] * 5,
        out_specs=(VMEM, VMEM),
        scratch_shapes=[
            pltpu.VMEM((Q_DEV * TLEN, D), BF16),
            pltpu.VMEM((D, D), BF16),
            pltpu.VMEM((D, D), BF16),
            pltpu.VMEM((D, D), BF16),
            pltpu.VMEM((D, D), BF16),
            pltpu.VMEM((Q_DEV, D), F32),
            pltpu.VMEM((DEVICES * BLOCK, 128), F32),
            pltpu.SemaphoreType.DMA((5,)),
        ],
        compiler_params=plain,
        name="self_stage",
    )(
        pair_image,
        text_states.reshape(Q_DEV * TLEN, D),
        w_self_q,
        w_self_k,
        w_self_v,
        w_self_o,
    )
    got = pl.pallas_call(
        exchange_kernel,
        out_shape=jax.ShapeDtypeStruct((DEVICES * BLOCK, 128), BF16),
        in_specs=[VMEM],
        out_specs=VMEM,
        scratch_shapes=[pltpu.SemaphoreType.DMA(())] * 3,
        compiler_params=pltpu.CompilerParams(
            collective_id=0, has_side_effects=True, vmem_limit_bytes=8 * 1024 * 1024
        ),
        name="exchange",
    )(send)
    back = pl.pallas_call(
        cross_kernel,
        out_shape=jax.ShapeDtypeStruct((DEVICES, 128), F32),
        in_specs=[VMEM, VMEM] + [ANY] * 6,
        out_specs=VMEM,
        scratch_shapes=[
            pltpu.VMEM((D, D), BF16),
            pltpu.VMEM((D, D), BF16),
            pltpu.VMEM((D, FF), BF16),
            pltpu.VMEM((FF, D), BF16),
            pltpu.VMEM((IMG_DEV, IMG_TOK, D), BF16),
            pltpu.VMEM((IMG_DEV, IMG_TOK, D), BF16),
            pltpu.VMEM((DEVICES * BLOCK, 128), F32),
            pltpu.VMEM((SLOTS, D), BF16),
            pltpu.VMEM((SORTED, D), BF16),
            pltpu.VMEM((SORTED, D), BF16),
            pltpu.VMEM((2, SLOTS, FF_STEP), BF16),
            pltpu.VMEM((SLOTS, D), F32),
            pltpu.SemaphoreType.DMA((4 + 2 * IMG_DEV,)),
        ],
        compiler_params=plain,
        name="cross_stage",
    )(got, itm_head, image_keys, image_values, w_cross_q, w_cross_o, w_up, w_down)
    return pl.pallas_call(
        return_kernel,
        out_shape=jax.ShapeDtypeStruct((Q_DEV, TOPK), F32),
        in_specs=[VMEM] * 6,
        out_specs=VMEM,
        scratch_shapes=[pltpu.VMEM((DEVICES, 1, 128), F32)]
        + [pltpu.SemaphoreType.DMA(())] * 3,
        compiler_params=pltpu.CompilerParams(
            collective_id=1, has_side_effects=True, vmem_limit_bytes=8 * 1024 * 1024
        ),
        name="give_back",
    )(
        back.reshape(DEVICES, 1, 128),
        meta,
        caption_aligned_vector,
        cluster_list,
        pair_image,
        pictures,
    )


def solution(mesh):
    sharded = ("gallery", "query")
    return jax.shard_map(
        local,
        mesh=mesh,
        in_specs=(
            P(sharded, None, None),
            P(sharded, None),
            P(sharded, None),
            P(sharded, None),
            P(sharded, None, None),
            P(sharded, None, None),
            P(sharded, None),
        )
        + (P(),) * 9,
        out_specs=P(sharded, None),
        check_vma=False,
    )
```

```python
import functools

import jax
import jax.numpy as jnp
from jax import lax
from jax.experimental import pallas as pl
from jax.experimental.pallas import tpu as pltpu
from jax.sharding import PartitionSpec as P

F32 = jnp.float32
BF16 = jnp.bfloat16
MESH = pl.DeviceIdType.MESH

HEADS = 12
HEAD = 64
D = 768
FF = 3072
TLEN = 32
Q_DEV = 32
TOPK = 16
IMG_DEV = 4
IMG_TOK = 577
CAP = 5
DEVICES = 128
MEMBERS = 4
PAIRS = Q_DEV * TOPK
SLOTS = DEVICES * CAP
CHUNKS = D // 128
BLOCK = 32
E = 256
NLIST = 8
PLANE = 8
PICS = 16
INFO = CAP * CHUNKS
TILE = 64
TILES = SLOTS // TILE + IMG_DEV - 1
SORTED = TILES * TILE
GROUP = 256
FF_STEP = 256

norm_epsilon = 1e-06
inverse_softness_factor = 1.0 / 0.07
VMEM_LIMIT = 56 * 1024 * 1024


def iota(shape, dimension):
    return lax.broadcasted_iota(jnp.int32, shape, dimension)


def dot(left, right, left_dim=1, right_dim=0):
    return lax.dot_general(
        left, right, (((left_dim,), (right_dim,)), ((), ())), preferred_element_type=F32
    )


def layer_norm(inputs):
    centered = inputs - jnp.mean(inputs, axis=-1, keepdims=True)
    variance = jnp.mean(centered * centered, axis=-1, keepdims=True)
    return centered * lax.rsqrt(variance + norm_epsilon)


def gelu(x):
    z = jnp.abs(x) * 0.7071067811865476
    t = 1.0 / (1.0 + 0.3275911 * z)
    poly = t * (
        0.254829592
        + t * (-0.284496736 + t * (1.421413741 + t * (-1.453152027 + t * 1.061405429)))
    )
    half_tail = 0.5 * poly * jnp.exp(-z * z)
    return x * jnp.where(x < 0, half_tail, 1.0 - half_tail)


def hot(marks):
    return marks.astype(F32).astype(BF16)


def pair_columns(pairs):
    spread = hot(iota((PAIRS, TOPK), 0) // Q_DEV == iota((PAIRS, TOPK), 1))
    place = iota((PAIRS, Q_DEV), 0) % Q_DEV == iota((PAIRS, Q_DEV), 1)

    def column(values):
        rows = dot(spread, values.astype(F32).astype(BF16))
        return jnp.sum(jnp.where(place, rows, 0.0), axis=1, keepdims=True)

    return column(pairs // IMG_DEV), column(pairs % IMG_DEV)


def turned(values):
    size = values.shape[0]
    eye = hot(iota((size, size), 0) == iota((size, size), 1))
    return dot(values.astype(F32).astype(BF16), eye, 0, 0)


def position():
    return lax.axis_index("gallery") * MEMBERS + lax.axis_index("query")


def place_of(device):
    return (device // MEMBERS, device % MEMBERS)


def block_of(device, rows):
    return pl.ds(pl.multiple_of(device * rows, rows), rows)


def greet_all(me):
    barrier = pltpu.get_barrier_semaphore()

    def greet(step, carry):
        pl.semaphore_signal(
            barrier, inc=1, device_id=place_of((me + step) % DEVICES), device_id_type=MESH
        )
        return carry

    lax.fori_loop(1, DEVICES, greet, 0)


def push_all(first, last, other_of, source_of, target, send_sem, got_sem):
    def push(step, carry):
        other = other_of(step)
        pltpu.make_async_remote_copy(
            src_ref=source_of(other),
            dst_ref=target,
            send_sem=send_sem,
            recv_sem=got_sem,
            device_id=place_of(other),
            device_id_type=MESH,
        ).start()
        return carry

    lax.fori_loop(first, last, push, 0)


def wait_all(view, sem):
    pltpu.make_async_copy(view, view, sem).wait()


def sort_slots(info):
    image = jnp.concatenate([info[:, slot : slot + 1] for slot in range(CAP)], axis=0)
    image = image.astype(jnp.int32) - 1
    image_marks = iota((SLOTS, 128), 1) == image
    earlier = hot(iota((SLOTS, SLOTS), 1) < iota((SLOTS, SLOTS), 0))
    counts = dot(earlier, hot(image_marks))
    sizes = jnp.sum(image_marks.astype(F32), axis=0, keepdims=True).astype(jnp.int32)
    tiles = (sizes + (TILE - 1)) // TILE
    lane = iota((1, 128), 1)
    starts = [jnp.int32(0)]
    for number in range(IMG_DEV - 1):
        starts.append(starts[-1] + jnp.sum(jnp.where(lane == number, tiles, 0)))
    offset = jnp.zeros((1, 128), F32)
    for number in range(1, IMG_DEV):
        offset = jnp.where(lane == number, (starts[number] * TILE).astype(F32), offset)
    target = jnp.sum(jnp.where(image_marks, counts + offset, 0.0), axis=1, keepdims=True)
    target = jnp.where(image >= 0, target, -1.0).astype(jnp.int32)
    return hot(iota((SLOTS, SORTED), 1) == target), starts


def contrast(caption, lists, pairs, pictures):
    lanes = DEVICES * PLANE
    high = dot(caption[:, 128:], pictures, 1, 1)
    scores = dot(caption[:, :128], pictures, 1, 1) + pltpu.roll(high, lanes - IMG_DEV, 1)
    scores = scores * inverse_softness_factor
    lane = iota((Q_DEV, lanes), 1)
    real = lane % PLANE < IMG_DEV
    image = jnp.where(real, lane // PLANE * IMG_DEV + lane % PLANE, -2)
    listed = image // 2 == lists[:, 0:1]
    for number in range(1, NLIST):
        listed = listed | (image // 2 == lists[:, number : number + 1])
    masked = jnp.where(listed, scores, -1e30)
    top = jnp.max(masked, axis=1, keepdims=True)
    sums = jnp.sum(jnp.where(listed, jnp.exp(masked - top), 0.0), axis=1, keepdims=True)
    itc_total = top + jnp.log(sums)
    place = iota((Q_DEV, TOPK), 1)
    offset = jnp.zeros((Q_DEV, TOPK), F32)
    for number in range(TOPK):
        chosen = jnp.sum(
            jnp.where(image == pairs[:, number : number + 1], scores, 0.0),
            axis=1,
            keepdims=True,
        )
        offset = jnp.where(place == number, chosen, offset)
    return offset - itc_total


def kernel(
    pair_ref, list_ref, caption_ref, picture_ref, head_ref,
    text_hbm, wq_hbm, wk_hbm, wv_hbm, wo_hbm, wcq_hbm, keys_hbm, values_hbm, wco_hbm, up_hbm,
    down_hbm, out_ref,
    text, wq, wk, wv, wo, wcq, keys, values, wco, up, down,
    first, wide, send, got, state, asked, context, hidden, total,
    picture_near, picture_mine, picture_all, margins, margins_got, offsets, sems, link_sems,
):
    me = position()
    targets = (text, wq, wk, wv, wo, wcq, keys, values, wco, up, down)
    sources = (
        text_hbm, wq_hbm, wk_hbm, wv_hbm, wo_hbm, wcq_hbm, keys_hbm, values_hbm, wco_hbm,
        up_hbm, down_hbm,
    )
    copies = [
        pltpu.make_async_copy(source, target, sems.at[number])
        for number, (source, target) in enumerate(zip(sources, targets))
    ]
    for copy in copies:
        copy.start()
    greet_all(me)

    pairs = pair_ref[...]
    owner, pick = pair_columns(pairs)
    lane = iota((PAIRS, DEVICES), 1)
    owner_marks = lane == owner.astype(jnp.int32)
    owner_hot = hot(owner_marks)
    earlier = hot(iota((PAIRS, PAIRS), 1) < iota((PAIRS, PAIRS), 0))
    counts = dot(earlier, owner_hot)
    rank = jnp.sum(jnp.where(owner_marks, counts, 0.0), axis=1, keepdims=True)
    rank = rank.astype(jnp.int32)
    query_lane = iota((PAIRS, 256), 1)
    query_of = iota((PAIRS, 256), 0) % Q_DEV
    query_hot = (query_lane == rank * Q_DEV + query_of) & (rank < CAP)
    slot_query = dot(owner_hot, hot(query_hot), 0, 0).astype(BF16)
    pick_hot = jnp.where(lane == rank, pick + 1.0, 0.0).astype(BF16)
    slot_pick = dot(owner_hot, pick_hot, 0, 0)
    wide[pl.ds(INFO, DEVICES, stride=BLOCK), :] = slot_pick
    wide[pl.ds(INFO + 1, DEVICES, stride=BLOCK), :] = jnp.zeros((DEVICES, 128), F32)

    pictures = picture_ref[...].astype(F32)
    pictures = jnp.concatenate(
        [pictures[:, :128], pictures[:, 128:], jnp.zeros((PLANE, 128), F32)], axis=0
    ).astype(BF16)
    near = 2 * MEMBERS
    corner = me // near * near
    own_near = block_of(me % near, PICS)
    picture_mine[...] = pictures
    picture_near[own_near, :] = pictures
    pl.semaphore_wait(pltpu.get_barrier_semaphore(), DEVICES - 1)
    push_all(
        1, near, lambda step: corner + (me + step) % near, lambda other: picture_mine,
        picture_near.at[own_near, :], link_sems.at[0], link_sems.at[1],
    )

    copies[0].wait()
    for n in range(Q_DEV):
        first[n : n + 1, :] = text[n * TLEN : n * TLEN + 16, :].astype(F32)[0:1, :]
    first_rows = first[...]
    copies[1].wait()
    query = dot(first_rows.astype(BF16), wq[...]).astype(BF16).astype(F32) * HEAD**-0.5
    copies[2].wait()
    copies[3].wait()
    head_mask = iota((16, D), 1) // HEAD == iota((16, D), 0)
    per_group = GROUP // TLEN
    own = iota((per_group * 16, GROUP), 0) // 16 == iota((per_group * 16, GROUP), 1) // TLEN
    contexts = []
    for group in range(Q_DEV // per_group):
        rows = text[group * GROUP : (group + 1) * GROUP, :]
        key_rows = dot(rows, wk[...]).astype(BF16)
        value_rows = dot(rows, wv[...]).astype(BF16)
        part = query[group * per_group : (group + 1) * per_group, :]
        spread = jnp.where(head_mask[None], part[:, None, :], 0.0)
        spread = spread.reshape(per_group * 16, D).astype(BF16)
        scores = jnp.where(own, dot(spread, key_rows, 1, 1), -1e30)
        exps = jnp.exp(scores - jnp.max(scores, axis=1, keepdims=True))
        weights = (exps / jnp.sum(exps, axis=1, keepdims=True)).astype(BF16)
        mixed = dot(weights, value_rows).reshape(per_group, 16, D)
        contexts.append(jnp.sum(jnp.where(head_mask[None], mixed, 0.0), axis=1))
    self_context = jnp.concatenate(contexts, axis=0).astype(BF16)
    copies[4].wait()
    leading = layer_norm(first_rows + dot(self_context, wo[...])).astype(BF16)
    for slot in range(CAP):
        rows = dot(slot_query[:, slot * Q_DEV : (slot + 1) * Q_DEV], leading)
        for chunk in range(CHUNKS):
            wide[pl.ds(slot * CHUNKS + chunk, DEVICES, stride=BLOCK), :] = rows[
                :, chunk * 128 : (chunk + 1) * 128
            ]
    send[...] = wide[...].astype(BF16)

    mine = block_of(me, BLOCK)
    own_copy = pltpu.make_async_copy(send.at[mine, :], got.at[mine, :], link_sems.at[2])
    own_copy.start()
    push_all(
        1, DEVICES, lambda step: (me + step) % DEVICES,
        lambda other: send.at[block_of(other, BLOCK), :],
        got.at[mine, :], link_sems.at[3], link_sems.at[4],
    )

    seven = pl.ds(0, (near - 1) * PICS)
    wait_all(picture_near.at[seven, :], link_sems.at[0])
    wait_all(picture_near.at[seven, :], link_sems.at[1])
    column = near * PLANE
    gathered = jnp.concatenate(
        [
            picture_near[number * PICS : (number + 1) * PICS, :].astype(F32)[:PLANE]
            for number in range(near)
        ],
        axis=0,
    ).astype(BF16)
    own_column = block_of(me // near, column)
    picture_all[own_column, :] = gathered
    push_all(
        1, DEVICES // near, lambda step: (me + step * near) % DEVICES,
        lambda other: picture_all.at[own_column, :],
        picture_all.at[own_column, :], link_sems.at[5], link_sems.at[6],
    )
    others = pl.ds(0, (DEVICES // near - 1) * column)
    wait_all(picture_all.at[others, :], link_sems.at[5])
    wait_all(picture_all.at[others, :], link_sems.at[6])
    image_of = turned(pairs // IMG_DEV) * IMG_DEV + turned(pairs % IMG_DEV)
    offset = contrast(
        caption_ref[...],
        turned(list_ref[...]).astype(jnp.int32),
        image_of.astype(jnp.int32),
        picture_all[...],
    )
    offsets[...] = offset.T

    own_copy.wait()
    most = pl.ds(0, (DEVICES - 1) * BLOCK)
    wait_all(send.at[most, :], link_sems.at[3])
    wait_all(got.at[most, :], link_sems.at[4])

    wide[...] = got[...].astype(F32)
    for slot in range(CAP):
        for chunk in range(CHUNKS):
            rows = wide[pl.ds(slot * CHUNKS + chunk, DEVICES, stride=BLOCK), :]
            state[
                slot * DEVICES : (slot + 1) * DEVICES, chunk * 128 : (chunk + 1) * 128
            ] = rows.astype(BF16)
    order, starts = sort_slots(wide[pl.ds(INFO, DEVICES, stride=BLOCK), :])
    copies[5].wait()
    query = (dot(state[...], wcq[...]).astype(BF16).astype(F32) * HEAD**-0.5).astype(BF16)
    asked[...] = dot(order, query, 0, 0).astype(BF16)
    copies[6].wait()
    copies[7].wait()
    lane_head = iota((1, 256), 1) // HEAD

    def attend(tile, carry):
        number = sum((tile >= start).astype(jnp.int32) for start in starts[1:])
        rows = pl.ds(pl.multiple_of(tile * TILE, TILE), TILE)
        for group in range(D // 256):
            columns = slice(group * 256, (group + 1) * 256)
            part = asked[rows, columns].astype(F32)
            spread = jnp.concatenate(
                [jnp.where(lane_head == head, part, 0.0) for head in range(4)], axis=0
            ).astype(BF16)
            scores = dot(spread, keys[number, :, columns], 1, 1)
            exps = jnp.exp(scores - jnp.max(scores, axis=1, keepdims=True))
            weight = 1.0 / jnp.sum(exps, axis=1, keepdims=True)
            mixed = dot(exps.astype(BF16), values[number, :, columns]) * weight
            joined = jnp.where(lane_head == 0, mixed[:TILE, :], 0.0)
            for head in range(1, 4):
                joined = jnp.where(
                    lane_head == head, mixed[head * TILE : (head + 1) * TILE, :], joined
                )
            context[rows, columns] = joined.astype(BF16)
        return carry

    lax.fori_loop(0, TILES, attend, 0)
    found = dot(order, context[...]).astype(BF16)
    copies[8].wait()
    crossed = layer_norm(state[...].astype(F32) + dot(found, wco[...])).astype(BF16)
    state[...] = crossed
    total[...] = crossed.astype(F32)

    copies[9].wait()
    copies[10].wait()

    def raise_step(step):
        columns = pl.ds(pl.multiple_of(step * FF_STEP, FF_STEP), FF_STEP)
        return gelu(dot(state[...], up[:, columns])).astype(BF16)

    def lower_step(step):
        rows = pl.ds(pl.multiple_of(step * FF_STEP, FF_STEP), FF_STEP)
        return dot(hidden[step % 2], down[rows, :])

    hidden[0] = raise_step(0)

    def feed(step, carry):
        total[...] += lower_step(step - 1)
        hidden[step % 2] = raise_step(step)
        return carry

    steps = FF // FF_STEP
    lax.fori_loop(1, steps, feed, 0)
    final = layer_norm(total[...] + lower_step(steps - 1)).astype(BF16)
    logits = dot(final, head_ref[...], 1, 1)
    margin = logits[:, 1:2] - logits[:, 0:1]
    back = jnp.zeros((DEVICES, 128), F32)
    back_lane = iota((DEVICES, 128), 1)
    for slot in range(CAP):
        back = jnp.where(
            back_lane == slot, margin[slot * DEVICES : (slot + 1) * DEVICES, :], back
        )
    margins[...] = back.reshape(DEVICES, 1, 128)

    own_back = pltpu.make_async_copy(margins.at[me], margins_got.at[me], link_sems.at[2])
    own_back.start()
    push_all(
        1, DEVICES, lambda step: (me + step) % DEVICES, lambda other: margins.at[other],
        margins_got.at[me], link_sems.at[7], link_sems.at[8],
    )
    own_back.wait()
    rest_of = pl.ds(0, DEVICES - 1)
    wait_all(margins.at[rest_of], link_sems.at[7])
    wait_all(margins_got.at[rest_of], link_sems.at[8])
    rest = margins_got[...].reshape(DEVICES, 128)
    chosen = jnp.zeros((PAIRS, 128), F32)
    for _ in range(3):
        piece = rest.astype(BF16)
        chosen = chosen + dot(owner_hot, piece)
        rest = rest - piece.astype(F32)
    chosen = jnp.sum(jnp.where(lane == rank, chosen, 0.0), axis=1, keepdims=True)
    query_place = iota((PAIRS, 128), 0) % Q_DEV == iota((PAIRS, 128), 1)
    placed = jnp.where(query_place, chosen, 0.0).reshape(TOPK, Q_DEV, 128)
    out_ref[...] = jnp.sum(placed, axis=1)[:, :Q_DEV] + offsets[...]


VMEM = pl.BlockSpec(memory_space=pltpu.VMEM)
ANY = pl.BlockSpec(memory_space=pl.ANY)


def local(
    text_states,
    caption_aligned_vector,
    cluster_list,
    pair_image,
    image_keys,
    image_values,
    picture_aligned_vector,
    w_self_q,
    w_self_k,
    w_self_v,
    w_self_o,
    w_cross_q,
    w_cross_o,
    w_up,
    w_down,
    itm_head,
):
    square = pltpu.VMEM((D, D), BF16)
    gallery = pltpu.VMEM((IMG_DEV, IMG_TOK, D), BF16)
    blocks = pltpu.VMEM((DEVICES * BLOCK, 128), BF16)
    sorted_rows = pltpu.VMEM((SORTED, D), BF16)
    margin_rows = pltpu.VMEM((DEVICES, 1, 128), F32)
    out = pl.pallas_call(
        kernel,
        out_shape=jax.ShapeDtypeStruct((TOPK, Q_DEV), F32),
        in_specs=[VMEM] * 5 + [ANY] * 11,
        out_specs=VMEM,
        scratch_shapes=[
            pltpu.VMEM((Q_DEV * TLEN, D), BF16),
            square,
            square,
            square,
            square,
            square,
            gallery,
            gallery,
            square,
            pltpu.VMEM((D, FF), BF16),
            pltpu.VMEM((FF, D), BF16),
            pltpu.VMEM((Q_DEV, D), F32),
            pltpu.VMEM((DEVICES * BLOCK, 128), F32),
            blocks,
            blocks,
            pltpu.VMEM((SLOTS, D), BF16),
            sorted_rows,
            sorted_rows,
            pltpu.VMEM((2, SLOTS, FF_STEP), BF16),
            pltpu.VMEM((SLOTS, D), F32),
            pltpu.VMEM((2 * MEMBERS * PICS, 128), BF16),
            pltpu.VMEM((PICS, 128), BF16),
            pltpu.VMEM((DEVICES * PLANE, 128), BF16),
            margin_rows,
            margin_rows,
            pltpu.VMEM((TOPK, Q_DEV), F32),
            pltpu.SemaphoreType.DMA((11,)),
            pltpu.SemaphoreType.DMA((9,)),
        ],
        compiler_params=pltpu.CompilerParams(
            collective_id=0, has_side_effects=True, vmem_limit_bytes=VMEM_LIMIT
        ),
        name="rerank_all",
    )(
        pair_image.T,
        cluster_list.T,
        caption_aligned_vector,
        picture_aligned_vector,
        itm_head.T,
        text_states.reshape(Q_DEV * TLEN, D),
        w_self_q,
        w_self_k,
        w_self_v,
        w_self_o,
        w_cross_q,
        image_keys,
        image_values,
        w_cross_o,
        w_up,
        w_down,
    )
    return out.T


def solution(mesh):
    sharded = ("gallery", "query")
    return jax.shard_map(
        local,
        mesh=mesh,
        in_specs=(
            P(sharded, None, None),
            P(sharded, None),
            P(sharded, None),
            P(sharded, None),
            P(sharded, None, None),
            P(sharded, None, None),
            P(sharded, None),
        )
        + (P(),) * 9,
        out_specs=P(sharded, None),
        check_vma=False,
    )
```

```python
import functools

import jax
import jax.numpy as jnp
from jax import lax
from jax.experimental import pallas as pl
from jax.experimental.pallas import tpu as pltpu
from jax.sharding import PartitionSpec as P

F32 = jnp.float32
BF16 = jnp.bfloat16
MESH = pl.DeviceIdType.MESH

HEADS = 12
HEAD = 64
D = 768
FF = 3072
TLEN = 32
Q_DEV = 32
TOPK = 16
IMG_DEV = 4
IMG_TOK = 577
CAP = 5
DEVICES = 128
MEMBERS = 4
PAIRS = Q_DEV * TOPK
SLOTS = DEVICES * CAP
CHUNKS = D // 128
BLOCK = 32
E = 256
NLIST = 8
PLANE = 8
PICS = 16
INFO = CAP * CHUNKS
TILE = 64
TILES = SLOTS // TILE + IMG_DEV - 1
SORTED = TILES * TILE
GROUP = 256
FF_STEP = 512

norm_epsilon = 1e-06
inverse_softness_factor = 1.0 / 0.07
VMEM_LIMIT = 56 * 1024 * 1024


def iota(shape, dimension):
    return lax.broadcasted_iota(jnp.int32, shape, dimension)


def dot(left, right, left_dim=1, right_dim=0):
    return lax.dot_general(
        left, right, (((left_dim,), (right_dim,)), ((), ())), preferred_element_type=F32
    )


def layer_norm(inputs):
    centered = inputs - jnp.mean(inputs, axis=-1, keepdims=True)
    variance = jnp.mean(centered * centered, axis=-1, keepdims=True)
    return centered * lax.rsqrt(variance + norm_epsilon)


def gelu(x):
    return 0.5 * x * (1.0 + lax.erf(x * 0.7071067811865476))


def hot(marks):
    return marks.astype(F32).astype(BF16)


def pair_columns(pairs):
    spread = hot(iota((PAIRS, TOPK), 0) // Q_DEV == iota((PAIRS, TOPK), 1))
    place = iota((PAIRS, Q_DEV), 0) % Q_DEV == iota((PAIRS, Q_DEV), 1)

    def column(values):
        rows = dot(spread, values.astype(F32).astype(BF16))
        return jnp.sum(jnp.where(place, rows, 0.0), axis=1, keepdims=True)

    return column(pairs // IMG_DEV), column(pairs % IMG_DEV)


def turned(values):
    size = values.shape[0]
    eye = hot(iota((size, size), 0) == iota((size, size), 1))
    return dot(values.astype(F32).astype(BF16), eye, 0, 0)


def position():
    return lax.axis_index("gallery") * MEMBERS + lax.axis_index("query")


def place_of(device):
    return (device // MEMBERS, device % MEMBERS)


def block_of(device, rows):
    return pl.ds(pl.multiple_of(device * rows, rows), rows)


def greet_all(me):
    barrier = pltpu.get_barrier_semaphore()

    def greet(step, carry):
        pl.semaphore_signal(
            barrier, inc=1, device_id=place_of((me + step) % DEVICES), device_id_type=MESH
        )
        return carry

    lax.fori_loop(1, DEVICES, greet, 0)


def push_all(first, last, other_of, source_of, target, send_sem, got_sem):
    def push(step, carry):
        other = other_of(step)
        pltpu.make_async_remote_copy(
            src_ref=source_of(other),
            dst_ref=target,
            send_sem=send_sem,
            recv_sem=got_sem,
            device_id=place_of(other),
            device_id_type=MESH,
        ).start()
        return carry

    lax.fori_loop(first, last, push, 0)


def wait_all(view, sem):
    pltpu.make_async_copy(view, view, sem).wait()


def sort_slots(info):
    image = jnp.concatenate([info[:, slot : slot + 1] for slot in range(CAP)], axis=0)
    image = image.astype(jnp.int32) - 1
    image_marks = iota((SLOTS, 128), 1) == image
    earlier = hot(iota((SLOTS, SLOTS), 1) < iota((SLOTS, SLOTS), 0))
    counts = dot(earlier, hot(image_marks))
    sizes = jnp.sum(image_marks.astype(F32), axis=0, keepdims=True).astype(jnp.int32)
    tiles = (sizes + (TILE - 1)) // TILE
    lane = iota((1, 128), 1)
    starts = [jnp.int32(0)]
    for number in range(IMG_DEV - 1):
        starts.append(starts[-1] + jnp.sum(jnp.where(lane == number, tiles, 0)))
    offset = jnp.zeros((1, 128), F32)
    for number in range(1, IMG_DEV):
        offset = jnp.where(lane == number, (starts[number] * TILE).astype(F32), offset)
    target = jnp.sum(jnp.where(image_marks, counts + offset, 0.0), axis=1, keepdims=True)
    target = jnp.where(image >= 0, target, -1.0).astype(jnp.int32)
    return hot(iota((SLOTS, SORTED), 1) == target), starts


def contrast(caption, lists, pairs, pictures):
    lanes = DEVICES * PLANE
    high = dot(caption[:, 128:], pictures, 1, 1)
    scores = dot(caption[:, :128], pictures, 1, 1) + pltpu.roll(high, lanes - IMG_DEV, 1)
    scores = scores * inverse_softness_factor
    lane = iota((Q_DEV, lanes), 1)
    real = lane % PLANE < IMG_DEV
    image = jnp.where(real, lane // PLANE * IMG_DEV + lane % PLANE, -2)
    listed = image // 2 == lists[:, 0:1]
    for number in range(1, NLIST):
        listed = listed | (image // 2 == lists[:, number : number + 1])
    masked = jnp.where(listed, scores, -1e30)
    top = jnp.max(masked, axis=1, keepdims=True)
    sums = jnp.sum(jnp.where(listed, jnp.exp(masked - top), 0.0), axis=1, keepdims=True)
    itc_total = top + jnp.log(sums)
    place = iota((Q_DEV, TOPK), 1)
    offset = jnp.zeros((Q_DEV, TOPK), F32)
    for number in range(TOPK):
        chosen = jnp.sum(
            jnp.where(image == pairs[:, number : number + 1], scores, 0.0),
            axis=1,
            keepdims=True,
        )
        offset = jnp.where(place == number, chosen, offset)
    return offset - itc_total


def kernel(
    pair_ref, list_ref, caption_ref, picture_ref, head_ref,
    text_hbm, wq_hbm, wk_hbm, wv_hbm, wo_hbm, wcq_hbm, keys_hbm, values_hbm, wco_hbm, up_hbm,
    down_hbm, out_ref,
    text, wq, wk, wv, wo, wcq, keys, values, wco, up, down,
    first, wide, send, got, state, asked, context, hidden,
    picture_near, picture_mine, picture_all, margins, by_place, near_margins, by_corner,
    margins_got, offsets, sems, link_sems,
):
    me = position()
    targets = (text, wq, wk, wv, wo, wcq, keys, values, wco, up, down)
    sources = (
        text_hbm, wq_hbm, wk_hbm, wv_hbm, wo_hbm, wcq_hbm, keys_hbm, values_hbm, wco_hbm,
        up_hbm, down_hbm,
    )
    copies = [
        pltpu.make_async_copy(source, target, sems.at[number])
        for number, (source, target) in enumerate(zip(sources, targets))
    ]
    for copy in copies:
        copy.start()
    greet_all(me)

    pairs = pair_ref[...]
    owner, pick = pair_columns(pairs)
    lane = iota((PAIRS, DEVICES), 1)
    owner_marks = lane == owner.astype(jnp.int32)
    owner_hot = hot(owner_marks)
    earlier = hot(iota((PAIRS, PAIRS), 1) < iota((PAIRS, PAIRS), 0))
    counts = dot(earlier, owner_hot)
    rank = jnp.sum(jnp.where(owner_marks, counts, 0.0), axis=1, keepdims=True)
    rank = rank.astype(jnp.int32)
    query_lane = iota((PAIRS, 256), 1)
    query_of = iota((PAIRS, 256), 0) % Q_DEV
    query_hot = (query_lane == rank * Q_DEV + query_of) & (rank < CAP)
    slot_query = dot(owner_hot, hot(query_hot), 0, 0).astype(BF16)
    pick_hot = jnp.where(lane == rank, pick + 1.0, 0.0).astype(BF16)
    slot_pick = dot(owner_hot, pick_hot, 0, 0)
    wide[pl.ds(INFO, DEVICES, stride=BLOCK), :] = slot_pick
    wide[pl.ds(INFO + 1, DEVICES, stride=BLOCK), :] = jnp.zeros((DEVICES, 128), F32)

    pictures = picture_ref[...].astype(F32)
    pictures = jnp.concatenate(
        [pictures[:, :128], pictures[:, 128:], jnp.zeros((PLANE, 128), F32)], axis=0
    ).astype(BF16)
    near = 2 * MEMBERS
    corner = me // near * near
    own_near = block_of(me % near, PICS)
    picture_mine[...] = pictures
    picture_near[own_near, :] = pictures
    pl.semaphore_wait(pltpu.get_barrier_semaphore(), DEVICES - 1)
    push_all(
        1, near, lambda step: corner + (me + step) % near, lambda other: picture_mine,
        picture_near.at[own_near, :], link_sems.at[0], link_sems.at[1],
    )

    copies[0].wait()
    for n in range(Q_DEV):
        first[n : n + 1, :] = text[n * TLEN : n * TLEN + 16, :].astype(F32)[0:1, :]
    first_rows = first[...]
    copies[1].wait()
    query = dot(first_rows.astype(BF16), wq[...]).astype(BF16).astype(F32) * HEAD**-0.5
    copies[2].wait()
    copies[3].wait()
    head_mask = iota((16, D), 1) // HEAD == iota((16, D), 0)
    per_group = GROUP // TLEN
    own = iota((per_group * 16, GROUP), 0) // 16 == iota((per_group * 16, GROUP), 1) // TLEN
    contexts = []
    for group in range(Q_DEV // per_group):
        rows = text[group * GROUP : (group + 1) * GROUP, :]
        key_rows = dot(rows, wk[...]).astype(BF16)
        value_rows = dot(rows, wv[...]).astype(BF16)
        part = query[group * per_group : (group + 1) * per_group, :]
        spread = jnp.where(head_mask[None], part[:, None, :], 0.0)
        spread = spread.reshape(per_group * 16, D).astype(BF16)
        scores = jnp.where(own, dot(spread, key_rows, 1, 1), -1e30)
        exps = jnp.exp(scores - jnp.max(scores, axis=1, keepdims=True))
        weights = (exps / jnp.sum(exps, axis=1, keepdims=True)).astype(BF16)
        mixed = dot(weights, value_rows).reshape(per_group, 16, D)
        contexts.append(jnp.sum(jnp.where(head_mask[None], mixed, 0.0), axis=1))
    self_context = jnp.concatenate(contexts, axis=0).astype(BF16)
    copies[4].wait()
    leading = layer_norm(first_rows + dot(self_context, wo[...])).astype(BF16)
    for slot in range(CAP):
        rows = dot(slot_query[:, slot * Q_DEV : (slot + 1) * Q_DEV], leading)
        for chunk in range(CHUNKS):
            wide[pl.ds(slot * CHUNKS + chunk, DEVICES, stride=BLOCK), :] = rows[
                :, chunk * 128 : (chunk + 1) * 128
            ]
    send[...] = wide[...].astype(BF16)

    mine = block_of(me, BLOCK)
    own_copy = pltpu.make_async_copy(send.at[mine, :], got.at[mine, :], link_sems.at[2])
    own_copy.start()
    push_all(
        1, DEVICES, lambda step: (me + step) % DEVICES,
        lambda other: send.at[block_of(other, BLOCK), :],
        got.at[mine, :], link_sems.at[3], link_sems.at[4],
    )

    seven = pl.ds(0, (near - 1) * PICS)
    wait_all(picture_near.at[seven, :], link_sems.at[0])
    wait_all(picture_near.at[seven, :], link_sems.at[1])
    column = near * PLANE
    gathered = jnp.concatenate(
        [
            picture_near[number * PICS : (number + 1) * PICS, :].astype(F32)[:PLANE]
            for number in range(near)
        ],
        axis=0,
    ).astype(BF16)
    own_column = block_of(me // near, column)
    picture_all[own_column, :] = gathered
    push_all(
        1, DEVICES // near, lambda step: (me + step * near) % DEVICES,
        lambda other: picture_all.at[own_column, :],
        picture_all.at[own_column, :], link_sems.at[5], link_sems.at[6],
    )
    others = pl.ds(0, (DEVICES // near - 1) * column)
    wait_all(picture_all.at[others, :], link_sems.at[5])
    wait_all(picture_all.at[others, :], link_sems.at[6])
    image_of = turned(pairs // IMG_DEV) * IMG_DEV + turned(pairs % IMG_DEV)
    offset = contrast(
        caption_ref[...],
        turned(list_ref[...]).astype(jnp.int32),
        image_of.astype(jnp.int32),
        picture_all[...],
    )
    offsets[...] = offset.T

    own_copy.wait()
    most = pl.ds(0, (DEVICES - 1) * BLOCK)
    wait_all(send.at[most, :], link_sems.at[3])
    wait_all(got.at[most, :], link_sems.at[4])

    wide[...] = got[...].astype(F32)
    for slot in range(CAP):
        for chunk in range(CHUNKS):
            rows = wide[pl.ds(slot * CHUNKS + chunk, DEVICES, stride=BLOCK), :]
            state[
                slot * DEVICES : (slot + 1) * DEVICES, chunk * 128 : (chunk + 1) * 128
            ] = rows.astype(BF16)
    order, starts = sort_slots(wide[pl.ds(INFO, DEVICES, stride=BLOCK), :])
    copies[5].wait()
    query = (dot(state[...], wcq[...]).astype(BF16).astype(F32) * HEAD**-0.5).astype(BF16)
    asked[...] = dot(order, query, 0, 0).astype(BF16)
    copies[6].wait()
    copies[7].wait()
    lane_head = iota((1, 256), 1) // HEAD

    for tile in range(TILES):
        number = sum((tile >= start).astype(jnp.int32) for start in starts[1:])
        rows = slice(tile * TILE, (tile + 1) * TILE)
        for group in range(D // 256):
            columns = slice(group * 256, (group + 1) * 256)
            part = asked[rows, columns].astype(F32)
            spread = jnp.concatenate(
                [jnp.where(lane_head == head, part, 0.0) for head in range(4)], axis=0
            ).astype(BF16)
            scores = dot(spread, keys[number, :, columns], 1, 1)
            exps = jnp.exp(scores - jnp.max(scores, axis=1, keepdims=True))
            weight = 1.0 / jnp.sum(exps, axis=1, keepdims=True)
            mixed = dot(exps.astype(BF16), values[number, :, columns]) * weight
            joined = jnp.where(lane_head == 0, mixed[:TILE, :], 0.0)
            for head in range(1, 4):
                joined = jnp.where(
                    lane_head == head, mixed[head * TILE : (head + 1) * TILE, :], joined
                )
            context[rows, columns] = joined.astype(BF16)

    found = dot(order, context[...]).astype(BF16)
    copies[8].wait()
    crossed = layer_norm(state[...].astype(F32) + dot(found, wco[...])).astype(BF16)
    state[...] = crossed

    copies[9].wait()
    for step in range(FF // FF_STEP):
        columns = slice(step * FF_STEP, (step + 1) * FF_STEP)
        hidden[:, columns] = gelu(dot(state[...], up[:, columns])).astype(BF16)
    copies[10].wait()
    final = layer_norm(state[...].astype(F32) + dot(hidden[...], down[...])).astype(BF16)
    logits = dot(final, head_ref[...], 1, 1)
    margin = logits[:, 1:2] - logits[:, 0:1]
    back = jnp.zeros((DEVICES, 128), F32)
    back_lane = iota((DEVICES, 128), 1)
    for slot in range(CAP):
        back = jnp.where(
            back_lane == slot, margin[slot * DEVICES : (slot + 1) * DEVICES, :], back
        )
    margins[...] = back

    corners = DEVICES // near
    my_place = me % near
    my_corner = me // near
    for place in range(near):
        by_place[place * corners : (place + 1) * corners, :] = margins[
            pl.ds(place, corners, stride=near), :
        ]
    own_row = block_of(my_place, corners)
    near_margins[own_row, :] = by_place[own_row, :]
    push_all(
        1, near, lambda step: corner + (me + step) % near,
        lambda other: by_place.at[block_of(other % near, corners), :],
        near_margins.at[own_row, :], link_sems.at[7], link_sems.at[8],
    )
    seven = pl.ds(0, (near - 1) * corners)
    wait_all(by_place.at[seven, :], link_sems.at[7])
    wait_all(near_margins.at[seven, :], link_sems.at[8])
    for place in range(corners):
        by_corner[place * near : (place + 1) * near, :] = near_margins[
            pl.ds(place, near, stride=corners), :
        ]
    own_row = block_of(my_corner, near)
    margins_got[own_row, :] = by_corner[own_row, :]
    push_all(
        1, corners, lambda step: (me + step * near) % DEVICES,
        lambda other: by_corner.at[block_of(other // near, near), :],
        margins_got.at[own_row, :], link_sems.at[9], link_sems.at[10],
    )
    others = pl.ds(0, (corners - 1) * near)
    wait_all(by_corner.at[others, :], link_sems.at[9])
    wait_all(margins_got.at[others, :], link_sems.at[10])
    rest = margins_got[...]
    chosen = jnp.zeros((PAIRS, 128), F32)
    for _ in range(3):
        piece = rest.astype(BF16)
        chosen = chosen + dot(owner_hot, piece)
        rest = rest - piece.astype(F32)
    chosen = jnp.sum(jnp.where(lane == rank, chosen, 0.0), axis=1, keepdims=True)
    query_place = iota((PAIRS, 128), 0) % Q_DEV == iota((PAIRS, 128), 1)
    placed = jnp.where(query_place, chosen, 0.0).reshape(TOPK, Q_DEV, 128)
    out_ref[...] = jnp.sum(placed, axis=1)[:, :Q_DEV] + offsets[...]


VMEM = pl.BlockSpec(memory_space=pltpu.VMEM)
ANY = pl.BlockSpec(memory_space=pl.ANY)


def local(
    text_states,
    caption_aligned_vector,
    cluster_list,
    pair_image,
    image_keys,
    image_values,
    picture_aligned_vector,
    w_self_q,
    w_self_k,
    w_self_v,
    w_self_o,
    w_cross_q,
    w_cross_o,
    w_up,
    w_down,
    itm_head,
):
    square = pltpu.VMEM((D, D), BF16)
    gallery = pltpu.VMEM((IMG_DEV, IMG_TOK, D), BF16)
    blocks = pltpu.VMEM((DEVICES * BLOCK, 128), BF16)
    sorted_rows = pltpu.VMEM((SORTED, D), BF16)
    margin_rows = pltpu.VMEM((DEVICES, 128), F32)
    out = pl.pallas_call(
        kernel,
        out_shape=jax.ShapeDtypeStruct((TOPK, Q_DEV), F32),
        in_specs=[VMEM] * 5 + [ANY] * 11,
        out_specs=VMEM,
        scratch_shapes=[
            pltpu.VMEM((Q_DEV * TLEN, D), BF16),
            square,
            square,
            square,
            square,
            square,
            gallery,
            gallery,
            square,
            pltpu.VMEM((D, FF), BF16),
            pltpu.VMEM((FF, D), BF16),
            pltpu.VMEM((Q_DEV, D), F32),
            pltpu.VMEM((DEVICES * BLOCK, 128), F32),
            blocks,
            blocks,
            pltpu.VMEM((SLOTS, D), BF16),
            sorted_rows,
            sorted_rows,
            pltpu.VMEM((SLOTS, FF), BF16),
            pltpu.VMEM((2 * MEMBERS * PICS, 128), BF16),
            pltpu.VMEM((PICS, 128), BF16),
            pltpu.VMEM((DEVICES * PLANE, 128), BF16),
            margin_rows,
            margin_rows,
            margin_rows,
            margin_rows,
            margin_rows,
            pltpu.VMEM((TOPK, Q_DEV), F32),
            pltpu.SemaphoreType.DMA((11,)),
            pltpu.SemaphoreType.DMA((11,)),
        ],
        compiler_params=pltpu.CompilerParams(
            collective_id=0, has_side_effects=True, vmem_limit_bytes=VMEM_LIMIT
        ),
        name="rerank_all",
    )(
        pair_image.T,
        cluster_list.T,
        caption_aligned_vector,
        picture_aligned_vector,
        itm_head.T,
        text_states.reshape(Q_DEV * TLEN, D),
        w_self_q,
        w_self_k,
        w_self_v,
        w_self_o,
        w_cross_q,
        image_keys,
        image_values,
        w_cross_o,
        w_up,
        w_down,
    )
    return out.T


def solution(mesh):
    sharded = ("gallery", "query")
    return jax.shard_map(
        local,
        mesh=mesh,
        in_specs=(
            P(sharded, None, None),
            P(sharded, None),
            P(sharded, None),
            P(sharded, None),
            P(sharded, None, None),
            P(sharded, None, None),
            P(sharded, None),
        )
        + (P(),) * 9,
        out_specs=P(sharded, None),
        check_vma=False,
    )
```

```python
import functools

import jax
import jax.numpy as jnp
from jax import lax
from jax.experimental import pallas as pl
from jax.experimental.pallas import tpu as pltpu
from jax.sharding import PartitionSpec as P

F32 = jnp.float32
BF16 = jnp.bfloat16
MESH = pl.DeviceIdType.MESH

HEADS = 12
HEAD = 64
D = 768
FF = 3072
TLEN = 32
Q_DEV = 32
TOPK = 16
IMG_DEV = 4
IMG_TOK = 577
CAP = 5
DEVICES = 128
MEMBERS = 4
PAIRS = Q_DEV * TOPK
SLOTS = DEVICES * CAP
CHUNKS = D // 128
BLOCK = 32
E = 256
NLIST = 8
PLANE = 8
PICS = 16
INFO = CAP * CHUNKS
TILE = 64
TURNS = 2
TILES = -(-(SLOTS // TILE + IMG_DEV - 1) // TURNS) * TURNS
SORTED = TILES * TILE
GROUP = 256
FF_STEP = 512

norm_epsilon = 1e-06
inverse_softness_factor = 1.0 / 0.07
VMEM_LIMIT = 56 * 1024 * 1024


def iota(shape, dimension):
    return lax.broadcasted_iota(jnp.int32, shape, dimension)


def dot(left, right, left_dim=1, right_dim=0):
    return lax.dot_general(
        left, right, (((left_dim,), (right_dim,)), ((), ())), preferred_element_type=F32
    )


def layer_norm(inputs):
    centered = inputs - jnp.mean(inputs, axis=-1, keepdims=True)
    variance = jnp.mean(centered * centered, axis=-1, keepdims=True)
    return centered * lax.rsqrt(variance + norm_epsilon)


def gelu(x):
    return 0.5 * x * (1.0 + lax.erf(x * 0.7071067811865476))


def hot(marks):
    return marks.astype(F32).astype(BF16)


def pair_columns(pairs):
    spread = hot(iota((PAIRS, TOPK), 0) // Q_DEV == iota((PAIRS, TOPK), 1))
    place = iota((PAIRS, Q_DEV), 0) % Q_DEV == iota((PAIRS, Q_DEV), 1)

    def column(values):
        rows = dot(spread, values.astype(F32).astype(BF16))
        return jnp.sum(jnp.where(place, rows, 0.0), axis=1, keepdims=True)

    return column(pairs // IMG_DEV), column(pairs % IMG_DEV)


def turned(values):
    size = values.shape[0]
    eye = hot(iota((size, size), 0) == iota((size, size), 1))
    return dot(values.astype(F32).astype(BF16), eye, 0, 0)


def position():
    return lax.axis_index("gallery") * MEMBERS + lax.axis_index("query")


def place_of(device):
    return (device // MEMBERS, device % MEMBERS)


def block_of(device, rows):
    return pl.ds(pl.multiple_of(device * rows, rows), rows)


def greet_all(me):
    barrier = pltpu.get_barrier_semaphore()

    def greet(step, carry):
        pl.semaphore_signal(
            barrier, inc=1, device_id=place_of((me + step) % DEVICES), device_id_type=MESH
        )
        return carry

    lax.fori_loop(1, DEVICES, greet, 0)


def push_all(first, last, other_of, source_of, target, send_sem, got_sem):
    def push(step, carry):
        other = other_of(step)
        pltpu.make_async_remote_copy(
            src_ref=source_of(other),
            dst_ref=target,
            send_sem=send_sem,
            recv_sem=got_sem,
            device_id=place_of(other),
            device_id_type=MESH,
        ).start()
        return carry

    lax.fori_loop(first, last, push, 0)


def wait_all(view, sem):
    pltpu.make_async_copy(view, view, sem).wait()


def by_image(raw, target):
    def turn(tokens):
        target[:, tokens, :] = jnp.transpose(raw[tokens].astype(F32), (1, 0, 2)).astype(BF16)

    def some(step, carry):
        turn(pl.ds(pl.multiple_of(step * 64, 64), 64))
        return carry

    whole = IMG_TOK // 64
    lax.fori_loop(0, whole, some, 0)
    turn(slice(whole * 64, IMG_TOK))


def sort_slots(info):
    image = jnp.concatenate([info[:, slot : slot + 1] for slot in range(CAP)], axis=0)
    image = image.astype(jnp.int32) - 1
    image_marks = iota((SLOTS, 128), 1) == image
    earlier = hot(iota((SLOTS, SLOTS), 1) < iota((SLOTS, SLOTS), 0))
    counts = dot(earlier, hot(image_marks))
    sizes = jnp.sum(image_marks.astype(F32), axis=0, keepdims=True).astype(jnp.int32)
    tiles = (sizes + (TILE - 1)) // TILE
    lane = iota((1, 128), 1)
    starts = [jnp.int32(0)]
    for number in range(IMG_DEV - 1):
        starts.append(starts[-1] + jnp.sum(jnp.where(lane == number, tiles, 0)))
    offset = jnp.zeros((1, 128), F32)
    for number in range(1, IMG_DEV):
        offset = jnp.where(lane == number, (starts[number] * TILE).astype(F32), offset)
    target = jnp.sum(jnp.where(image_marks, counts + offset, 0.0), axis=1, keepdims=True)
    target = jnp.where(image >= 0, target, -1.0).astype(jnp.int32)
    return hot(iota((SLOTS, SORTED), 1) == target), starts


def contrast(caption, lists, pairs, pictures):
    lanes = DEVICES * PLANE
    high = dot(caption[:, 128:], pictures, 1, 1)
    scores = dot(caption[:, :128], pictures, 1, 1) + pltpu.roll(high, lanes - IMG_DEV, 1)
    scores = scores * inverse_softness_factor
    lane = iota((Q_DEV, lanes), 1)
    real = lane % PLANE < IMG_DEV
    image = jnp.where(real, lane // PLANE * IMG_DEV + lane % PLANE, -2)
    listed = image // 2 == lists[:, 0:1]
    for number in range(1, NLIST):
        listed = listed | (image // 2 == lists[:, number : number + 1])
    masked = jnp.where(listed, scores, -1e30)
    top = jnp.max(masked, axis=1, keepdims=True)
    sums = jnp.sum(jnp.where(listed, jnp.exp(masked - top), 0.0), axis=1, keepdims=True)
    itc_total = top + jnp.log(sums)
    place = iota((Q_DEV, TOPK), 1)
    offset = jnp.zeros((Q_DEV, TOPK), F32)
    for number in range(TOPK):
        chosen = jnp.sum(
            jnp.where(image == pairs[:, number : number + 1], scores, 0.0),
            axis=1,
            keepdims=True,
        )
        offset = jnp.where(place == number, chosen, offset)
    return offset - itc_total


def kernel(
    pair_ref, list_ref, caption_ref, picture_ref, head_ref,
    text_hbm, wq_hbm, wk_hbm, wv_hbm, wo_hbm, wcq_hbm, keys_hbm, values_hbm, wco_hbm, up_hbm,
    down_hbm, out_ref,
    text, wq, wk, wv, wo, wcq, raw, wco, up, down, keys, values,
    first, wide, send, got, state, asked, context, hidden,
    picture_near, picture_mine, picture_all, margins, by_place, near_margins, by_corner,
    margins_got, sems, link_sems,
):
    me = position()
    targets = (text, wq, wk, wv, wo, wcq, raw, raw, wco, up, down)
    sources = (
        text_hbm, wq_hbm, wk_hbm, wv_hbm, wo_hbm, wcq_hbm, keys_hbm, values_hbm, wco_hbm,
        up_hbm, down_hbm,
    )
    copies = [
        pltpu.make_async_copy(source, target, sems.at[number])
        for number, (source, target) in enumerate(zip(sources, targets))
    ]
    for copy in copies[:7] + copies[8:]:
        copy.start()
    greet_all(me)

    pairs = pair_ref[...]
    owner, pick = pair_columns(pairs)
    lane = iota((PAIRS, DEVICES), 1)
    owner_marks = lane == owner.astype(jnp.int32)
    owner_hot = hot(owner_marks)
    earlier = hot(iota((PAIRS, PAIRS), 1) < iota((PAIRS, PAIRS), 0))
    counts = dot(earlier, owner_hot)
    rank = jnp.sum(jnp.where(owner_marks, counts, 0.0), axis=1, keepdims=True)
    rank = rank.astype(jnp.int32)
    query_lane = iota((PAIRS, 256), 1)
    query_of = iota((PAIRS, 256), 0) % Q_DEV
    query_hot = (query_lane == rank * Q_DEV + query_of) & (rank < CAP)
    slot_query = dot(owner_hot, hot(query_hot), 0, 0).astype(BF16)
    pick_hot = jnp.where(lane == rank, pick + 1.0, 0.0).astype(BF16)
    slot_pick = dot(owner_hot, pick_hot, 0, 0)
    wide[pl.ds(INFO, DEVICES, stride=BLOCK), :] = slot_pick
    wide[pl.ds(INFO + 1, DEVICES, stride=BLOCK), :] = jnp.zeros((DEVICES, 128), F32)

    pictures = picture_ref[...].astype(F32)
    pictures = jnp.concatenate(
        [pictures[:, :128], pictures[:, 128:], jnp.zeros((PLANE, 128), F32)], axis=0
    ).astype(BF16)
    near = 2 * MEMBERS
    corner = me // near * near
    own_near = block_of(me % near, PICS)
    picture_mine[...] = pictures
    picture_near[own_near, :] = pictures

    copies[0].wait()
    for n in range(Q_DEV):
        first[n : n + 1, :] = text[n * TLEN : n * TLEN + 16, :].astype(F32)[0:1, :]
    first_rows = first[...]
    copies[1].wait()
    query = dot(first_rows.astype(BF16), wq[...]).astype(BF16).astype(F32) * HEAD**-0.5
    copies[2].wait()
    copies[3].wait()
    head_mask = iota((16, D), 1) // HEAD == iota((16, D), 0)
    per_group = GROUP // TLEN
    own = iota((per_group * 16, GROUP), 0) // 16 == iota((per_group * 16, GROUP), 1) // TLEN
    contexts = []
    for group in range(Q_DEV // per_group):
        rows = text[group * GROUP : (group + 1) * GROUP, :]
        key_rows = dot(rows, wk[...]).astype(BF16)
        value_rows = dot(rows, wv[...]).astype(BF16)
        part = query[group * per_group : (group + 1) * per_group, :]
        spread = jnp.where(head_mask[None], part[:, None, :], 0.0)
        spread = spread.reshape(per_group * 16, D).astype(BF16)
        scores = jnp.where(own, dot(spread, key_rows, 1, 1), -1e30)
        exps = jnp.exp(scores - jnp.max(scores, axis=1, keepdims=True))
        weights = (exps / jnp.sum(exps, axis=1, keepdims=True)).astype(BF16)
        mixed = dot(weights, value_rows).reshape(per_group, 16, D)
        contexts.append(jnp.sum(jnp.where(head_mask[None], mixed, 0.0), axis=1))
    self_context = jnp.concatenate(contexts, axis=0).astype(BF16)
    copies[4].wait()
    leading = layer_norm(first_rows + dot(self_context, wo[...])).astype(BF16)
    for slot in range(CAP):
        rows = dot(slot_query[:, slot * Q_DEV : (slot + 1) * Q_DEV], leading)
        for chunk in range(CHUNKS):
            wide[pl.ds(slot * CHUNKS + chunk, DEVICES, stride=BLOCK), :] = rows[
                :, chunk * 128 : (chunk + 1) * 128
            ]
    send[...] = wide[...].astype(BF16)

    pl.semaphore_wait(pltpu.get_barrier_semaphore(), DEVICES - 1)
    mine = block_of(me, BLOCK)
    own_copy = pltpu.make_async_copy(send.at[mine, :], got.at[mine, :], link_sems.at[2])
    own_copy.start()
    push_all(
        1, DEVICES, lambda step: (me + step) % DEVICES,
        lambda other: send.at[block_of(other, BLOCK), :],
        got.at[mine, :], link_sems.at[3], link_sems.at[4],
    )

    push_all(
        1, near, lambda step: corner + (me + step) % near, lambda other: picture_mine,
        picture_near.at[own_near, :], link_sems.at[0], link_sems.at[1],
    )

    copies[6].wait()
    by_image(raw, keys)
    copies[7].start()
    copies[7].wait()
    by_image(raw, values)

    seven = pl.ds(0, (near - 1) * PICS)
    wait_all(picture_near.at[seven, :], link_sems.at[0])
    wait_all(picture_near.at[seven, :], link_sems.at[1])
    column = near * PLANE
    gathered = jnp.concatenate(
        [
            picture_near[number * PICS : (number + 1) * PICS, :].astype(F32)[:PLANE]
            for number in range(near)
        ],
        axis=0,
    ).astype(BF16)
    own_column = block_of(me // near, column)
    picture_all[own_column, :] = gathered
    push_all(
        1, DEVICES // near, lambda step: (me + step * near) % DEVICES,
        lambda other: picture_all.at[own_column, :],
        picture_all.at[own_column, :], link_sems.at[5], link_sems.at[6],
    )
    own_copy.wait()
    most = pl.ds(0, (DEVICES - 1) * BLOCK)
    wait_all(send.at[most, :], link_sems.at[3])
    wait_all(got.at[most, :], link_sems.at[4])

    wide[...] = got[...].astype(F32)
    for slot in range(CAP):
        for chunk in range(CHUNKS):
            rows = wide[pl.ds(slot * CHUNKS + chunk, DEVICES, stride=BLOCK), :]
            state[
                slot * DEVICES : (slot + 1) * DEVICES, chunk * 128 : (chunk + 1) * 128
            ] = rows.astype(BF16)
    order, starts = sort_slots(wide[pl.ds(INFO, DEVICES, stride=BLOCK), :])
    copies[5].wait()
    query = (dot(state[...], wcq[...]).astype(BF16).astype(F32) * HEAD**-0.5).astype(BF16)
    asked[...] = dot(order, query, 0, 0).astype(BF16)
    lane_head = iota((1, 256), 1) // HEAD

    def attend(turn, carry):
        for turn_tile in range(TILES // TURNS):
            tile = turn * (TILES // TURNS) + turn_tile
            number = sum((tile >= start).astype(jnp.int32) for start in starts[1:])
            rows = pl.ds(pl.multiple_of(tile * TILE, TILE), TILE)
            for group in range(D // 256):
                columns = slice(group * 256, (group + 1) * 256)
                part = asked[rows, columns].astype(F32)
                spread = jnp.concatenate(
                    [jnp.where(lane_head == head, part, 0.0) for head in range(4)], axis=0
                ).astype(BF16)
                scores = dot(spread, keys[number, :, columns], 1, 1)
                exps = jnp.exp(scores - jnp.max(scores, axis=1, keepdims=True))
                weight = 1.0 / jnp.sum(exps, axis=1, keepdims=True)
                mixed = dot(exps.astype(BF16), values[number, :, columns]) * weight
                joined = jnp.where(lane_head == 0, mixed[:TILE, :], 0.0)
                for head in range(1, 4):
                    joined = jnp.where(
                        lane_head == head, mixed[head * TILE : (head + 1) * TILE, :], joined
                    )
                context[rows, columns] = joined.astype(BF16)
        return carry

    lax.fori_loop(0, TURNS, attend, 0)

    found = dot(order, context[...]).astype(BF16)
    copies[8].wait()
    crossed = layer_norm(state[...].astype(F32) + dot(found, wco[...])).astype(BF16)
    state[...] = crossed

    copies[9].wait()
    for step in range(FF // FF_STEP):
        columns = slice(step * FF_STEP, (step + 1) * FF_STEP)
        hidden[:, columns] = gelu(dot(state[...], up[:, columns])).astype(BF16)
    copies[10].wait()
    final = layer_norm(state[...].astype(F32) + dot(hidden[...], down[...])).astype(BF16)
    logits = dot(final, head_ref[...], 1, 1)
    margin = logits[:, 1:2] - logits[:, 0:1]
    back = jnp.zeros((DEVICES, 128), F32)
    back_lane = iota((DEVICES, 128), 1)
    for slot in range(CAP):
        back = jnp.where(
            back_lane == slot, margin[slot * DEVICES : (slot + 1) * DEVICES, :], back
        )
    margins[...] = back

    corners = DEVICES // near
    my_place = me % near
    my_corner = me // near
    for place in range(near):
        by_place[place * corners : (place + 1) * corners, :] = margins[
            pl.ds(place, corners, stride=near), :
        ]
    own_row = block_of(my_place, corners)
    near_margins[own_row, :] = by_place[own_row, :]
    push_all(
        1, near, lambda step: corner + (me + step) % near,
        lambda other: by_place.at[block_of(other % near, corners), :],
        near_margins.at[own_row, :], link_sems.at[7], link_sems.at[8],
    )
    distant = pl.ds(0, (DEVICES // near - 1) * column)
    wait_all(picture_all.at[distant, :], link_sems.at[5])
    wait_all(picture_all.at[distant, :], link_sems.at[6])
    image_of = turned(pairs // IMG_DEV) * IMG_DEV + turned(pairs % IMG_DEV)
    offset = contrast(
        caption_ref[...],
        turned(list_ref[...]).astype(jnp.int32),
        image_of.astype(jnp.int32),
        picture_all[...],
    )
    offset = offset.T
    seven = pl.ds(0, (near - 1) * corners)
    wait_all(by_place.at[seven, :], link_sems.at[7])
    wait_all(near_margins.at[seven, :], link_sems.at[8])
    for place in range(corners):
        by_corner[place * near : (place + 1) * near, :] = near_margins[
            pl.ds(place, near, stride=corners), :
        ]
    own_row = block_of(my_corner, near)
    margins_got[own_row, :] = by_corner[own_row, :]
    push_all(
        1, corners, lambda step: (me + step * near) % DEVICES,
        lambda other: by_corner.at[block_of(other // near, near), :],
        margins_got.at[own_row, :], link_sems.at[9], link_sems.at[10],
    )
    others = pl.ds(0, (corners - 1) * near)
    wait_all(by_corner.at[others, :], link_sems.at[9])
    wait_all(margins_got.at[others, :], link_sems.at[10])
    rest = margins_got[...]
    chosen = jnp.zeros((PAIRS, 128), F32)
    for _ in range(3):
        piece = rest.astype(BF16)
        chosen = chosen + dot(owner_hot, piece)
        rest = rest - piece.astype(F32)
    chosen = jnp.sum(jnp.where(lane == rank, chosen, 0.0), axis=1, keepdims=True)
    query_place = iota((PAIRS, 128), 0) % Q_DEV == iota((PAIRS, 128), 1)
    placed = jnp.where(query_place, chosen, 0.0).reshape(TOPK, Q_DEV, 128)
    out_ref[...] = jnp.sum(placed, axis=1)[:, :Q_DEV] + offset


VMEM = pl.BlockSpec(memory_space=pltpu.VMEM)
ANY = pl.BlockSpec(memory_space=pl.ANY)


def local(
    text_states,
    caption_aligned_vector,
    cluster_list,
    pair_image,
    image_keys,
    image_values,
    picture_aligned_vector,
    w_self_q,
    w_self_k,
    w_self_v,
    w_self_o,
    w_cross_q,
    w_cross_o,
    w_up,
    w_down,
    itm_head,
):
    square = pltpu.VMEM((D, D), BF16)
    gallery = pltpu.VMEM((IMG_DEV, IMG_TOK, D), BF16)
    by_token = pltpu.VMEM((IMG_TOK, IMG_DEV, D), BF16)
    blocks = pltpu.VMEM((DEVICES * BLOCK, 128), BF16)
    sorted_rows = pltpu.VMEM((SORTED, D), BF16)
    margin_rows = pltpu.VMEM((DEVICES, 128), F32)
    out = pl.pallas_call(
        kernel,
        out_shape=jax.ShapeDtypeStruct((TOPK, Q_DEV), F32),
        in_specs=[VMEM] * 5 + [ANY] * 11,
        out_specs=VMEM,
        scratch_shapes=[
            pltpu.VMEM((Q_DEV * TLEN, D), BF16),
            square,
            square,
            square,
            square,
            square,
            by_token,
            square,
            pltpu.VMEM((D, FF), BF16),
            pltpu.VMEM((FF, D), BF16),
            gallery,
            gallery,
            pltpu.VMEM((Q_DEV, D), F32),
            pltpu.VMEM((DEVICES * BLOCK, 128), F32),
            blocks,
            blocks,
            pltpu.VMEM((SLOTS, D), BF16),
            sorted_rows,
            sorted_rows,
            pltpu.VMEM((SLOTS, FF), BF16),
            pltpu.VMEM((2 * MEMBERS * PICS, 128), BF16),
            pltpu.VMEM((PICS, 128), BF16),
            pltpu.VMEM((DEVICES * PLANE, 128), BF16),
            margin_rows,
            margin_rows,
            margin_rows,
            margin_rows,
            margin_rows,
            pltpu.SemaphoreType.DMA((11,)),
            pltpu.SemaphoreType.DMA((11,)),
        ],
        compiler_params=pltpu.CompilerParams(
            collective_id=0, has_side_effects=True, vmem_limit_bytes=VMEM_LIMIT
        ),
        name="rerank_all",
    )(
        pair_image.T,
        cluster_list.T,
        caption_aligned_vector,
        picture_aligned_vector,
        itm_head.T,
        text_states.reshape(Q_DEV * TLEN, D),
        w_self_q,
        w_self_k,
        w_self_v,
        w_self_o,
        w_cross_q,
        jnp.transpose(image_keys, (1, 0, 2)),
        jnp.transpose(image_values, (1, 0, 2)),
        w_cross_o,
        w_up,
        w_down,
    )
    return out.T


def solution(mesh):
    sharded = ("gallery", "query")
    return jax.shard_map(
        local,
        mesh=mesh,
        in_specs=(
            P(sharded, None, None),
            P(sharded, None),
            P(sharded, None),
            P(sharded, None),
            P(sharded, None, None),
            P(sharded, None, None),
            P(sharded, None),
        )
        + (P(),) * 9,
        out_specs=P(sharded, None),
        check_vma=False,
    )
```

```python
import functools

import jax
import jax.numpy as jnp
from jax import lax
from jax.experimental import pallas as pl
from jax.experimental.pallas import tpu as pltpu
from jax.sharding import PartitionSpec as P

F32 = jnp.float32
BF16 = jnp.bfloat16
MESH = pl.DeviceIdType.MESH

HEADS = 12
HEAD = 64
D = 768
FF = 3072
TLEN = 32
Q_DEV = 32
TOPK = 16
IMG_DEV = 4
IMG_TOK = 577
CAP = 5
DEVICES = 128
MEMBERS = 4
PAIRS = Q_DEV * TOPK
SLOTS = DEVICES * CAP
CHUNKS = D // 128
BLOCK = 32
E = 256
NLIST = 8
PLANE = 8
PICS = 16
INFO = CAP * CHUNKS
TILE = 64
TURNS = 2
TILES = -(-(SLOTS // TILE + IMG_DEV - 1) // TURNS) * TURNS
SORTED = TILES * TILE
GROUP = 256
FF_STEP = 512

norm_epsilon = 1e-06
inverse_softness_factor = 1.0 / 0.07
VMEM_LIMIT = 56 * 1024 * 1024


def iota(shape, dimension):
    return lax.broadcasted_iota(jnp.int32, shape, dimension)


def dot(left, right, left_dim=1, right_dim=0):
    return lax.dot_general(
        left, right, (((left_dim,), (right_dim,)), ((), ())), preferred_element_type=F32
    )


def layer_norm(inputs):
    centered = inputs - jnp.mean(inputs, axis=-1, keepdims=True)
    variance = jnp.mean(centered * centered, axis=-1, keepdims=True)
    return centered * lax.rsqrt(variance + norm_epsilon)


def gelu(x):
    return 0.5 * x * (1.0 + lax.erf(x * 0.7071067811865476))


def hot(marks):
    return marks.astype(F32).astype(BF16)


def pair_columns(pairs):
    spread = hot(iota((PAIRS, TOPK), 0) // Q_DEV == iota((PAIRS, TOPK), 1))
    place = iota((PAIRS, Q_DEV), 0) % Q_DEV == iota((PAIRS, Q_DEV), 1)

    def column(values):
        rows = dot(spread, values.astype(F32).astype(BF16))
        return jnp.sum(jnp.where(place, rows, 0.0), axis=1, keepdims=True)

    return column(pairs // IMG_DEV), column(pairs % IMG_DEV)


def turned(values):
    size = values.shape[0]
    eye = hot(iota((size, size), 0) == iota((size, size), 1))
    return dot(values.astype(F32).astype(BF16), eye, 0, 0)


def position():
    return lax.axis_index("gallery") * MEMBERS + lax.axis_index("query")


def place_of(device):
    return (lax.div(device, MEMBERS), lax.rem(device, MEMBERS))


def block_of(device, rows):
    return pl.ds(pl.multiple_of(device * rows, rows), rows)


def greet_all(me):
    barrier = pltpu.get_barrier_semaphore()

    def greet(step, carry):
        pl.semaphore_signal(
            barrier, inc=1, device_id=place_of(lax.rem(me + step, DEVICES)), device_id_type=MESH
        )
        return carry

    lax.fori_loop(1, DEVICES, greet, 0)


def push_all(first, last, other_of, source_of, target, send_sem, got_sem):
    def push(step, carry):
        other = other_of(step)
        pltpu.make_async_remote_copy(
            src_ref=source_of(other),
            dst_ref=target,
            send_sem=send_sem,
            recv_sem=got_sem,
            device_id=place_of(other),
            device_id_type=MESH,
        ).start()
        return carry

    lax.fori_loop(first, last, push, 0)


def wait_all(view, sem):
    pltpu.make_async_copy(view, view, sem).wait()


def by_image(raw, target):
    def turn(tokens):
        target[:, tokens, :] = jnp.transpose(raw[tokens].astype(F32), (1, 0, 2)).astype(BF16)

    def some(step, carry):
        turn(pl.ds(pl.multiple_of(step * 64, 64), 64))
        return carry

    whole = IMG_TOK // 64
    lax.fori_loop(0, whole, some, 0)
    turn(slice(whole * 64, IMG_TOK))


def sort_slots(info):
    image = jnp.concatenate([info[:, slot : slot + 1] for slot in range(CAP)], axis=0)
    image = image.astype(jnp.int32) - 1
    image_marks = iota((SLOTS, 128), 1) == image
    earlier = hot(iota((SLOTS, SLOTS), 1) < iota((SLOTS, SLOTS), 0))
    counts = dot(earlier, hot(image_marks))
    sizes = jnp.sum(image_marks.astype(F32), axis=0, keepdims=True).astype(jnp.int32)
    tiles = (sizes + (TILE - 1)) // TILE
    lane = iota((1, 128), 1)
    starts = [jnp.int32(0)]
    for number in range(IMG_DEV - 1):
        starts.append(starts[-1] + jnp.sum(jnp.where(lane == number, tiles, 0)))
    offset = jnp.zeros((1, 128), F32)
    for number in range(1, IMG_DEV):
        offset = jnp.where(lane == number, (starts[number] * TILE).astype(F32), offset)
    target = jnp.sum(jnp.where(image_marks, counts + offset, 0.0), axis=1, keepdims=True)
    target = jnp.where(image >= 0, target, -1.0).astype(jnp.int32)
    return hot(iota((SLOTS, SORTED), 1) == target), starts


def contrast(caption, lists, pairs, pictures):
    lanes = DEVICES * PLANE
    high = dot(caption[:, 128:], pictures, 1, 1)
    scores = dot(caption[:, :128], pictures, 1, 1) + pltpu.roll(high, lanes - IMG_DEV, 1)
    scores = scores * inverse_softness_factor
    lane = iota((Q_DEV, lanes), 1)
    real = lane % PLANE < IMG_DEV
    image = jnp.where(real, lane // PLANE * IMG_DEV + lane % PLANE, -2)
    listed = image // 2 == lists[:, 0:1]
    for number in range(1, NLIST):
        listed = listed | (image // 2 == lists[:, number : number + 1])
    masked = jnp.where(listed, scores, -1e30)
    top = jnp.max(masked, axis=1, keepdims=True)
    sums = jnp.sum(jnp.where(listed, jnp.exp(masked - top), 0.0), axis=1, keepdims=True)
    itc_total = top + jnp.log(sums)
    place = iota((Q_DEV, TOPK), 1)
    offset = jnp.zeros((Q_DEV, TOPK), F32)
    for number in range(TOPK):
        chosen = jnp.sum(
            jnp.where(image == pairs[:, number : number + 1], scores, 0.0),
            axis=1,
            keepdims=True,
        )
        offset = jnp.where(place == number, chosen, offset)
    return offset - itc_total


def kernel(
    pair_ref, list_ref, caption_ref, picture_ref, head_ref,
    text_hbm, wq_hbm, wk_hbm, wv_hbm, wo_hbm, wcq_hbm, keys_hbm, values_hbm, wco_hbm, up_hbm,
    down_hbm, out_ref,
    text, wq, wk, wv, wo, wcq, raw, wco, up, down, keys, values,
    first, wide, send, got, state, asked, context, hidden,
    picture_near, picture_mine, picture_all, margins, by_place, near_margins, by_corner,
    margins_got, sems, link_sems,
):
    me = position()
    targets = (text, wq, wk, wv, wo, wcq, raw, raw, wco, up, down)
    sources = (
        text_hbm, wq_hbm, wk_hbm, wv_hbm, wo_hbm, wcq_hbm, keys_hbm, values_hbm, wco_hbm,
        up_hbm, down_hbm,
    )
    copies = [
        pltpu.make_async_copy(source, target, sems.at[number])
        for number, (source, target) in enumerate(zip(sources, targets))
    ]
    for copy in copies[:7] + copies[8:]:
        copy.start()
    greet_all(me)

    pairs = pair_ref[...]
    owner, pick = pair_columns(pairs)
    lane = iota((PAIRS, DEVICES), 1)
    owner_marks = lane == owner.astype(jnp.int32)
    owner_hot = hot(owner_marks)
    earlier = hot(iota((PAIRS, PAIRS), 1) < iota((PAIRS, PAIRS), 0))
    counts = dot(earlier, owner_hot)
    rank = jnp.sum(jnp.where(owner_marks, counts, 0.0), axis=1, keepdims=True)
    rank = rank.astype(jnp.int32)
    query_lane = iota((PAIRS, 256), 1)
    query_of = iota((PAIRS, 256), 0) % Q_DEV
    query_hot = (query_lane == rank * Q_DEV + query_of) & (rank < CAP)
    slot_query = dot(owner_hot, hot(query_hot), 0, 0).astype(BF16)
    pick_hot = jnp.where(lane == rank, pick + 1.0, 0.0).astype(BF16)
    slot_pick = dot(owner_hot, pick_hot, 0, 0)
    wide[pl.ds(INFO, DEVICES, stride=BLOCK), :] = slot_pick
    wide[pl.ds(INFO + 1, DEVICES, stride=BLOCK), :] = jnp.zeros((DEVICES, 128), F32)

    pictures = picture_ref[...].astype(F32)
    pictures = jnp.concatenate(
        [pictures[:, :128], pictures[:, 128:], jnp.zeros((PLANE, 128), F32)], axis=0
    ).astype(BF16)
    near = 2 * MEMBERS
    corner = me // near * near
    own_near = block_of(me % near, PICS)
    picture_mine[...] = pictures
    picture_near[own_near, :] = pictures

    copies[0].wait()
    for n in range(Q_DEV):
        first[n : n + 1, :] = text[n * TLEN : n * TLEN + 16, :].astype(F32)[0:1, :]
    first_rows = first[...]
    copies[1].wait()
    query = dot(first_rows.astype(BF16), wq[...]).astype(BF16).astype(F32) * HEAD**-0.5
    copies[2].wait()
    copies[3].wait()
    head_mask = iota((16, D), 1) // HEAD == iota((16, D), 0)
    per_group = GROUP // TLEN
    own = iota((per_group * 16, GROUP), 0) // 16 == iota((per_group * 16, GROUP), 1) // TLEN
    contexts = []
    for group in range(Q_DEV // per_group):
        rows = text[group * GROUP : (group + 1) * GROUP, :]
        key_rows = dot(rows, wk[...]).astype(BF16)
        value_rows = dot(rows, wv[...]).astype(BF16)
        part = query[group * per_group : (group + 1) * per_group, :]
        spread = jnp.where(head_mask[None], part[:, None, :], 0.0)
        spread = spread.reshape(per_group * 16, D).astype(BF16)
        scores = jnp.where(own, dot(spread, key_rows, 1, 1), -1e30)
        exps = jnp.exp(scores - jnp.max(scores, axis=1, keepdims=True))
        weights = (exps / jnp.sum(exps, axis=1, keepdims=True)).astype(BF16)
        mixed = dot(weights, value_rows).reshape(per_group, 16, D)
        contexts.append(jnp.sum(jnp.where(head_mask[None], mixed, 0.0), axis=1))
    self_context = jnp.concatenate(contexts, axis=0).astype(BF16)
    copies[4].wait()
    leading = layer_norm(first_rows + dot(self_context, wo[...])).astype(BF16)
    for slot in range(CAP):
        rows = dot(slot_query[:, slot * Q_DEV : (slot + 1) * Q_DEV], leading)
        for chunk in range(CHUNKS):
            wide[pl.ds(slot * CHUNKS + chunk, DEVICES, stride=BLOCK), :] = rows[
                :, chunk * 128 : (chunk + 1) * 128
            ]
    send[...] = wide[...].astype(BF16)

    pl.semaphore_wait(pltpu.get_barrier_semaphore(), DEVICES - 1)
    mine = block_of(me, BLOCK)
    own_copy = pltpu.make_async_copy(send.at[mine, :], got.at[mine, :], link_sems.at[2])
    own_copy.start()
    push_all(
        1, DEVICES, lambda step: lax.rem(me + step * 37, DEVICES),
        lambda other: send.at[block_of(other, BLOCK), :],
        got.at[mine, :], link_sems.at[3], link_sems.at[4],
    )

    push_all(
        1, near, lambda step: corner + lax.rem(me + step, near), lambda other: picture_mine,
        picture_near.at[own_near, :], link_sems.at[0], link_sems.at[1],
    )

    copies[6].wait()
    by_image(raw, keys)
    copies[7].start()
    copies[7].wait()
    by_image(raw, values)

    seven = pl.ds(0, (near - 1) * PICS)
    wait_all(picture_near.at[seven, :], link_sems.at[0])
    wait_all(picture_near.at[seven, :], link_sems.at[1])
    column = near * PLANE
    gathered = jnp.concatenate(
        [
            picture_near[number * PICS : (number + 1) * PICS, :].astype(F32)[:PLANE]
            for number in range(near)
        ],
        axis=0,
    ).astype(BF16)
    own_column = block_of(me // near, column)
    picture_all[own_column, :] = gathered
    push_all(
        1, DEVICES // near, lambda step: lax.rem(me + step * near, DEVICES),
        lambda other: picture_all.at[own_column, :],
        picture_all.at[own_column, :], link_sems.at[5], link_sems.at[6],
    )
    own_copy.wait()
    most = pl.ds(0, (DEVICES - 1) * BLOCK)
    wait_all(send.at[most, :], link_sems.at[3])
    wait_all(got.at[most, :], link_sems.at[4])

    wide[...] = got[...].astype(F32)
    for slot in range(CAP):
        for chunk in range(CHUNKS):
            rows = wide[pl.ds(slot * CHUNKS + chunk, DEVICES, stride=BLOCK), :]
            state[
                slot * DEVICES : (slot + 1) * DEVICES, chunk * 128 : (chunk + 1) * 128
            ] = rows.astype(BF16)
    order, starts = sort_slots(wide[pl.ds(INFO, DEVICES, stride=BLOCK), :])
    copies[5].wait()
    query = (dot(state[...], wcq[...]).astype(BF16).astype(F32) * HEAD**-0.5).astype(BF16)
    asked[...] = dot(order, query, 0, 0).astype(BF16)
    lane_head = iota((1, 256), 1) // HEAD

    def attend(turn, carry):
        for turn_tile in range(TILES // TURNS):
            tile = turn * (TILES // TURNS) + turn_tile
            number = sum((tile >= start).astype(jnp.int32) for start in starts[1:])
            rows = pl.ds(pl.multiple_of(tile * TILE, TILE), TILE)
            for group in range(D // 256):
                columns = slice(group * 256, (group + 1) * 256)
                part = asked[rows, columns].astype(F32)
                spread = jnp.concatenate(
                    [jnp.where(lane_head == head, part, 0.0) for head in range(4)], axis=0
                ).astype(BF16)
                scores = dot(spread, keys[number, :, columns], 1, 1)
                exps = jnp.exp(scores - jnp.max(scores, axis=1, keepdims=True))
                weight = 1.0 / jnp.sum(exps, axis=1, keepdims=True)
                mixed = dot(exps.astype(BF16), values[number, :, columns]) * weight
                joined = jnp.where(lane_head == 0, mixed[:TILE, :], 0.0)
                for head in range(1, 4):
                    joined = jnp.where(
                        lane_head == head, mixed[head * TILE : (head + 1) * TILE, :], joined
                    )
                context[rows, columns] = joined.astype(BF16)
        return carry

    lax.fori_loop(0, TURNS, attend, 0)

    found = dot(order, context[...]).astype(BF16)
    copies[8].wait()
    crossed = layer_norm(state[...].astype(F32) + dot(found, wco[...])).astype(BF16)
    state[...] = crossed

    copies[9].wait()
    for step in range(FF // FF_STEP):
        columns = slice(step * FF_STEP, (step + 1) * FF_STEP)
        hidden[:, columns] = gelu(dot(state[...], up[:, columns])).astype(BF16)
    copies[10].wait()
    final = layer_norm(state[...].astype(F32) + dot(hidden[...], down[...])).astype(BF16)
    logits = dot(final, head_ref[...], 1, 1)
    margin = logits[:, 1:2] - logits[:, 0:1]
    back = jnp.zeros((DEVICES, 128), F32)
    back_lane = iota((DEVICES, 128), 1)
    for slot in range(CAP):
        back = jnp.where(
            back_lane == slot, margin[slot * DEVICES : (slot + 1) * DEVICES, :], back
        )
    margins[...] = back

    corners = DEVICES // near
    my_place = me % near
    my_corner = me // near
    for place in range(near):
        by_place[place * corners : (place + 1) * corners, :] = margins[
            pl.ds(place, corners, stride=near), :
        ]
    own_row = block_of(my_place, corners)
    near_margins[own_row, :] = by_place[own_row, :]
    push_all(
        1, near, lambda step: corner + lax.rem(me + step, near),
        lambda other: by_place.at[block_of(other % near, corners), :],
        near_margins.at[own_row, :], link_sems.at[7], link_sems.at[8],
    )
    distant = pl.ds(0, (DEVICES // near - 1) * column)
    wait_all(picture_all.at[distant, :], link_sems.at[5])
    wait_all(picture_all.at[distant, :], link_sems.at[6])
    image_of = turned(pairs // IMG_DEV) * IMG_DEV + turned(pairs % IMG_DEV)
    offset = contrast(
        caption_ref[...],
        turned(list_ref[...]).astype(jnp.int32),
        image_of.astype(jnp.int32),
        picture_all[...],
    )
    offset = offset.T
    seven = pl.ds(0, (near - 1) * corners)
    wait_all(by_place.at[seven, :], link_sems.at[7])
    wait_all(near_margins.at[seven, :], link_sems.at[8])
    for place in range(corners):
        by_corner[place * near : (place + 1) * near, :] = near_margins[
            pl.ds(place, near, stride=corners), :
        ]
    own_row = block_of(my_corner, near)
    margins_got[own_row, :] = by_corner[own_row, :]
    push_all(
        1, corners, lambda step: lax.rem(me + step * near, DEVICES),
        lambda other: by_corner.at[block_of(other // near, near), :],
        margins_got.at[own_row, :], link_sems.at[9], link_sems.at[10],
    )
    others = pl.ds(0, (corners - 1) * near)
    wait_all(by_corner.at[others, :], link_sems.at[9])
    wait_all(margins_got.at[others, :], link_sems.at[10])
    rest = margins_got[...]
    chosen = jnp.zeros((PAIRS, 128), F32)
    for _ in range(3):
        piece = rest.astype(BF16)
        chosen = chosen + dot(owner_hot, piece)
        rest = rest - piece.astype(F32)
    chosen = jnp.sum(jnp.where(lane == rank, chosen, 0.0), axis=1, keepdims=True)
    query_place = iota((PAIRS, 128), 0) % Q_DEV == iota((PAIRS, 128), 1)
    placed = jnp.where(query_place, chosen, 0.0).reshape(TOPK, Q_DEV, 128)
    out_ref[...] = jnp.sum(placed, axis=1)[:, :Q_DEV] + offset


VMEM = pl.BlockSpec(memory_space=pltpu.VMEM)
ANY = pl.BlockSpec(memory_space=pl.ANY)


def local(
    text_states,
    caption_aligned_vector,
    cluster_list,
    pair_image,
    image_keys,
    image_values,
    picture_aligned_vector,
    w_self_q,
    w_self_k,
    w_self_v,
    w_self_o,
    w_cross_q,
    w_cross_o,
    w_up,
    w_down,
    itm_head,
):
    square = pltpu.VMEM((D, D), BF16)
    gallery = pltpu.VMEM((IMG_DEV, IMG_TOK, D), BF16)
    by_token = pltpu.VMEM((IMG_TOK, IMG_DEV, D), BF16)
    blocks = pltpu.VMEM((DEVICES * BLOCK, 128), BF16)
    sorted_rows = pltpu.VMEM((SORTED, D), BF16)
    margin_rows = pltpu.VMEM((DEVICES, 128), F32)
    out = pl.pallas_call(
        kernel,
        out_shape=jax.ShapeDtypeStruct((TOPK, Q_DEV), F32),
        in_specs=[VMEM] * 5 + [ANY] * 11,
        out_specs=VMEM,
        scratch_shapes=[
            pltpu.VMEM((Q_DEV * TLEN, D), BF16),
            square,
            square,
            square,
            square,
            square,
            by_token,
            square,
            pltpu.VMEM((D, FF), BF16),
            pltpu.VMEM((FF, D), BF16),
            gallery,
            gallery,
            pltpu.VMEM((Q_DEV, D), F32),
            pltpu.VMEM((DEVICES * BLOCK, 128), F32),
            blocks,
            blocks,
            pltpu.VMEM((SLOTS, D), BF16),
            sorted_rows,
            sorted_rows,
            pltpu.VMEM((SLOTS, FF), BF16),
            pltpu.VMEM((2 * MEMBERS * PICS, 128), BF16),
            pltpu.VMEM((PICS, 128), BF16),
            pltpu.VMEM((DEVICES * PLANE, 128), BF16),
            margin_rows,
            margin_rows,
            margin_rows,
            margin_rows,
            margin_rows,
            pltpu.SemaphoreType.DMA((11,)),
            pltpu.SemaphoreType.DMA((11,)),
        ],
        compiler_params=pltpu.CompilerParams(
            collective_id=0, has_side_effects=True, vmem_limit_bytes=VMEM_LIMIT
        ),
        name="rerank_all",
    )(
        pair_image.T,
        cluster_list.T,
        caption_aligned_vector,
        picture_aligned_vector,
        itm_head.T,
        text_states.reshape(Q_DEV * TLEN, D),
        w_self_q,
        w_self_k,
        w_self_v,
        w_self_o,
        w_cross_q,
        jnp.transpose(image_keys, (1, 0, 2)),
        jnp.transpose(image_values, (1, 0, 2)),
        w_cross_o,
        w_up,
        w_down,
    )
    return out.T


def solution(mesh):
    sharded = ("gallery", "query")
    return jax.shard_map(
        local,
        mesh=mesh,
        in_specs=(
            P(sharded, None, None),
            P(sharded, None),
            P(sharded, None),
            P(sharded, None),
            P(sharded, None, None),
            P(sharded, None, None),
            P(sharded, None),
        )
        + (P(),) * 9,
        out_specs=P(sharded, None),
        check_vma=False,
    )
```
